32 devices in a mesh: group: 2 (over y), ctx: 4 (over z), tp: 2 (over x), rep: 2 (over core).
Axes of the slice: x: 2, y: 2, z: 4, core: 2. Of those that a mesh axis runs over, the one named last changes fastest.
Arguments:
- tokens: bfloat16 [1024, 8192], P(('group', 'ctx')), parts along dimension 0, may hold values from -6 to 6
- adapter_down: bfloat16 [32, 8192, 48], P(('group', 'ctx', 'rep')), parts along dimension 0, may hold values from -0.0625 to 0.0625
- adapter_query: bfloat16 [32, 16, 8, 8, 128], P(('group', 'ctx'), None, ('tp', 'rep')), parts along dimension 0, may hold values from -1.5 to 1.5
- adapter_keyvalue: bfloat16 [32, 16, 2, 8, 128], P(('group', 'ctx'), None, None, ('tp', 'rep')), parts along dimension 0, may hold values from -1.5 to 1.5
- query_base: bfloat16 [1024, 8, 8, 128], P(('group', 'ctx'), ('tp', 'rep')), parts along dimension 0, may hold values from -8 to 8
- keyvalue_base: bfloat16 [1024, 2, 8, 128], P(('group', 'ctx'), None, ('tp', 'rep')), parts along dimension 0, may hold values from -6 to 6
- cached_keys: bfloat16 [4096, 8, 128], P(('group', 'ctx'), ('tp', 'rep')), parts along dimension 0, may hold values from -8 to 8
- cached_values: bfloat16 [4096, 8, 128], P(('group', 'ctx'), ('tp', 'rep')), parts along dimension 0, may hold values from -6 to 6
- adapter_slot: int32 [8, 128], P(('group', 'ctx')), parts along dimension 0, may hold values from 0 to 3, never falling along the last dimension, each value on 1 to 64 neighbouring positions
- cached_length: int32 [8], P('group'), parts along dimension 0, may hold values from 1 to 512, 1280 in all
Outputs:
- attended: bfloat16 [1024, 8, 8, 128], P(('group', 'ctx'), ('tp', 'rep')), parts along dimension 0
The draws below stay inside these ranges and needn't reach their ends.
There are 2 independent parts, one for each index of `group`. The reference program is written for one: setup_inputs(seed, part) draws one part's arguments, and reference() takes and returns one part's arrays. A program takes and returns all parts, laid end to end along the dimension named above; each array names one. Nothing has to cross between parts.
Inputs may be any that keep to these rules, and one draw needn't show every extreme that they name: `adapter_slot`: non-decreasing along each row; every row uses each of its 4 adapters. `cached_length`: some shard is full.
All inputs are finite; a program needn't handle non-finite values.
Results may differ from the reference program's by a relative error of at most 0.012.
Values may be sent and summed in bfloat16 or wider, within the bound.
A program may use at most 64 MiB of HBM per device.

```python
import math
import jax
import jax.numpy as jnp
import numpy as np
from jax import lax

D = 8192
KV_HEADS = 8
HEAD_DIM = 128
RANK = 16
TOK_DEV = 128
CACHE_DEV = 512
GROUP = 8
SLOTS = 4
ADAPTERS = 16
SPAN = 512
CACHE = 2048


def draw_query_base(key, part):
    key = jax.random.fold_in(key, 7)
    array_shape = (SPAN, KV_HEADS, GROUP, HEAD_DIM)
    values = jnp.clip(2.0 * jax.random.normal(key, array_shape, jnp.float32), -8.0, 8.0)
    return values.astype(jnp.bfloat16)


def draw_cached_keys(key, part):
    key = jax.random.fold_in(key, 11)
    array_shape = (CACHE, KV_HEADS, HEAD_DIM)
    values = jnp.clip(jax.random.normal(key, array_shape, jnp.float32), -8.0, 8.0)
    return values.astype(jnp.bfloat16)


def levels(own_key, dims, shards, low, high):
    def one(dim, blocks):
        draws = jax.random.uniform(jax.random.fold_in(jax.random.fold_in(own_key, 6), dim), (blocks,), jnp.float32, low / len(shards), high / len(shards))
        return jnp.repeat(jnp.exp(draws), dims[dim] // blocks).reshape((-1,) + (1,) * (len(dims) - dim - 1))

    gain = one(*shards[0])
    for cut in shards[1:]:
        gain = gain * one(*cut)
    return gain


def split_up(count, total, bound, skew):
    weights = [(1 << 20) // math.isqrt(standing ** skew) + 1 for standing in range(2, count + 1)]
    spare, given = total - bound - (count - 1), [1] * (count - 1)
    while spare > 0:
        movable = [i for i in range(count - 1) if given[i] < bound]
        pool, remaining = sum([weights[i] for i in movable]), spare
        for i in movable:
            more = min(bound - given[i], max(1, remaining * weights[i] // pool), spare)
            given[i] = given[i] + more
            spare = spare - more
    return np.array([bound] + given)


def uneven(rng, amount, total, reach, skew):
    if amount == 2:
        one = jax.random.randint(rng, (), max(1, total - reach), min(reach, total - 1) + 1)
        return jnp.stack([one, total - one])
    sizes = jnp.asarray(split_up(amount, total, reach, skew), jnp.int32)
    couples = (amount - 1) // 2
    source_of, sink = sizes[1:1 + 2 * couples:2], sizes[2:2 + 2 * couples:2]
    room = jnp.minimum(source_of - 1, reach - sink)
    passed = jax.random.randint(jax.random.fold_in(rng, 1), (couples,), 0, 1 << 20) % (room + 1)
    sizes = sizes.at[1:1 + 2 * couples:2].set(source_of - passed).at[2:2 + 2 * couples:2].set(sink + passed)
    return sizes[jax.random.permutation(jax.random.fold_in(rng, 2), amount)]


def normal_values(own_key, extent, deviation, bound, split=(), kind=jnp.bfloat16):
    factor_of = levels(own_key, extent, split, -0.22, 0.18) if split else 1.0
    values = jax.random.normal(own_key, extent, jnp.float32) * deviation * factor_of
    return jnp.minimum(jnp.maximum(values, -bound), bound).astype(kind)


def setup_inputs(seed: int = 0, part: int = 0) -> dict:
    streams_of = jax.random.split(jax.random.key(seed), 11)
    part_splits = jax.random.split(jax.random.fold_in(streams_of[10], part), 11)
    tokens = normal_values(part_splits[0], (SPAN, D), 1.0, 6.0, ((0, 4),))
    adapter_down = normal_values(part_splits[1], (ADAPTERS, D, 3 * RANK), D ** -0.5, 0.0625, ((0, 8),))
    adapter_query = normal_values(part_splits[2], (ADAPTERS, RANK, KV_HEADS, GROUP, HEAD_DIM), RANK ** -0.5, 1.5, ((0, 4), (2, 4)))
    adapter_keyvalue = normal_values(part_splits[3], (ADAPTERS, RANK, 2, KV_HEADS, HEAD_DIM), RANK ** -0.5, 1.5, ((0, 4), (3, 4)))
    query_base = draw_query_base(jax.random.fold_in(jax.random.fold_in(streams_of[10], part), 71), part)
    keyvalue_base = normal_values(part_splits[5], (SPAN, 2, KV_HEADS, HEAD_DIM), 1.0, 6.0, ((0, 4), (2, 4)))
    cached_keys = draw_cached_keys(jax.random.fold_in(jax.random.fold_in(streams_of[10], part), 71), part)
    cached_values = normal_values(part_splits[7], (CACHE, KV_HEADS, HEAD_DIM), 1.0, 6.0, ((0, 4), (1, 4)))
    adapter_slot = jax.vmap(lambda own: jnp.searchsorted(jnp.cumsum(uneven(own, SLOTS, TOK_DEV, TOK_DEV // 2, 0)), jnp.arange(TOK_DEV), side="right"))(jax.random.split(part_splits[8], (SPAN // TOK_DEV))).reshape((SPAN // TOK_DEV, TOK_DEV)).astype(jnp.int32)
    cached_length = uneven(part_splits[9], CACHE // CACHE_DEV, CACHE * 5 // 8, CACHE_DEV, 2).astype(jnp.int32)
    return dict(tokens=tokens, adapter_down=adapter_down, adapter_query=adapter_query, adapter_keyvalue=adapter_keyvalue, query_base=query_base, keyvalue_base=keyvalue_base, cached_keys=cached_keys, cached_values=cached_values, adapter_slot=adapter_slot, cached_length=cached_length)


def reference(tokens, adapter_down, adapter_query, adapter_keyvalue, query_base, keyvalue_base, cached_keys, cached_values, adapter_slot, cached_length):
    shard_count = SPAN // TOK_DEV

    def adapt_shard(shard_items):
        token_rows, down_part, query_up, keyvalue_up, base_query, base_keyvalue, slot_ids = shard_items
        shrunk = jnp.einsum("td,sdk->stk", token_rows.astype(jnp.float32), down_part.astype(jnp.float32)).astype(jnp.bfloat16)
        selector = slot_ids[None, :] == jnp.arange(SLOTS, dtype=jnp.int32)[:, None]
        masked = jnp.where(selector[:, :, None], shrunk, jnp.zeros_like(shrunk))
        masked = lax.optimization_barrier(masked).astype(jnp.float32)
        delta_query = jnp.einsum("str,srhgd->thgd", masked[:, :, :RANK], query_up.astype(jnp.float32))
        query_rows = (base_query.astype(jnp.float32) + delta_query).astype(jnp.bfloat16)
        keyvalue_part = masked[:, :, RANK:].reshape(SLOTS, TOK_DEV, 2, RANK)
        delta_keyvalue = jnp.einsum("stcr,srchd->tchd", keyvalue_part, keyvalue_up.astype(jnp.float32))
        fresh_rows = (base_keyvalue.astype(jnp.float32) + delta_keyvalue).astype(jnp.bfloat16)
        return query_rows, fresh_rows

    query_all, fresh_all = lax.map(adapt_shard, (
        tokens.reshape(shard_count, TOK_DEV, D),
        adapter_down.reshape(shard_count, SLOTS, D, 3 * RANK),
        adapter_query.reshape(shard_count, SLOTS, RANK, KV_HEADS, GROUP, HEAD_DIM),
        adapter_keyvalue.reshape(shard_count, SLOTS, RANK, 2, KV_HEADS, HEAD_DIM),
        query_base.reshape(shard_count, TOK_DEV, KV_HEADS, GROUP, HEAD_DIM),
        keyvalue_base.reshape(shard_count, TOK_DEV, 2, KV_HEADS, HEAD_DIM),
        adapter_slot))
    fresh_all = fresh_all.reshape(SPAN, 2, KV_HEADS, HEAD_DIM)
    key_block = jnp.concatenate([cached_keys, fresh_all[:, 0]], axis=0)
    value_block = jnp.concatenate([cached_values, fresh_all[:, 1]], axis=0)
    key_block = lax.optimization_barrier(key_block).astype(jnp.float32)
    value_block = lax.optimization_barrier(value_block).astype(jnp.float32)
    slot_position = jnp.arange(CACHE, dtype=jnp.int32)
    cache_valid = (slot_position % CACHE_DEV) < cached_length[slot_position // CACHE_DEV]
    span_index = jnp.arange(SPAN, dtype=jnp.int32)
    score_scale = HEAD_DIM ** -0.5

    def attend(shard_items):
        query_rows, shard = shard_items
        query_position = shard * TOK_DEV + jnp.arange(TOK_DEV, dtype=jnp.int32)
        visible = jnp.concatenate([
            jnp.broadcast_to(cache_valid[None, :], (TOK_DEV, CACHE)),
            span_index[None, :] <= query_position[:, None]], axis=1)
        query_rows = lax.optimization_barrier(query_rows).astype(jnp.float32)
        scores = jnp.einsum("thgd,lhd->hgtl", query_rows, key_block) * score_scale
        row_max = jnp.max(jnp.where(visible, scores, -jnp.inf), axis=-1, keepdims=True)
        weights = jnp.where(visible, jnp.exp(scores - row_max), 0.0)
        denominator = jnp.sum(weights, axis=-1)
        rounded = lax.optimization_barrier(weights.astype(jnp.bfloat16)).astype(jnp.float32)
        output = jnp.einsum("hgtl,lhd->hgtd", rounded, value_block) / denominator[..., None]
        return jnp.transpose(output, (2, 0, 1, 3)).astype(jnp.bfloat16)

    attended = lax.map(attend, (query_all, jnp.arange(shard_count, dtype=jnp.int32)))
    return attended.reshape(SPAN, KV_HEADS, GROUP, HEAD_DIM)
```

```python
import functools

import jax
import jax.numpy as jnp
from jax import lax
from jax.experimental import pallas as pl
from jax.experimental.pallas import tpu as pltpu
from jax.sharding import PartitionSpec as P

FILL = -1e30
MESH = pl.DeviceIdType.MESH
TILE = 256
F32 = jnp.float32
BF16 = jnp.bfloat16


def iota(shape, dim):
    return lax.broadcasted_iota(jnp.int32, shape, dim)


def dot(a, b, ca=1, cb=0):
    return lax.dot_general(a, b, (((ca,), (cb,)), ((), ())), preferred_element_type=F32)


def kernel(
    n, heads, groups, slots, rank,
    tok_hbm, down_hbm, aq_ref, akv_ref, qb_ref, kvb_ref, ck_hbm, cv_hbm, slot_ref, len_ref,
    out_ref,
    tok_v, down_v, raw, kv, q, acc, top, total, xch, local_sem,
    send_rc, recv_rc, send_rf, recv_rf, send_lc, recv_lc, send_x, recv_x,
):
    me = lax.axis_index("ctx")
    rep = lax.axis_index("rep")
    toks = tok_v.shape[0]
    cached = ck_hbm.shape[0] // heads
    rows_all = cached + toks
    width = 3 * rank
    own_slots = down_hbm.shape[0] // width
    hd = q.shape[2]
    q_rows = toks * groups

    load_k = pltpu.make_async_copy(ck_hbm, raw.at[0], local_sem.at[0])
    load_v = pltpu.make_async_copy(cv_hbm, raw.at[1], local_sem.at[1])
    load_t = pltpu.make_async_copy(tok_hbm, tok_v, local_sem.at[2])
    load_d = pltpu.make_async_copy(down_hbm, down_v, local_sem.at[3])
    for load in (load_k, load_v, load_t, load_d):
        load.start()

    barrier = pltpu.get_barrier_semaphore()
    pl.semaphore_signal(barrier, inc=1, device_id={"rep": 1 - rep}, device_id_type=MESH)

    @pl.when(me > 0)
    def _():
        pl.semaphore_signal(barrier, inc=1, device_id={"ctx": me - 1}, device_id_type=MESH)

    @pl.when(me < n - 1)
    def _():
        pl.semaphore_signal(barrier, inc=1, device_id={"ctx": me + 1}, device_id_type=MESH)

    neighbours = 1 + jnp.where(me > 0, 1, 0) + jnp.where(me < n - 1, 1, 0)

    def cached_right(src):
        part = kv.at[src, :, :, pl.ds(0, cached)]
        return pltpu.make_async_remote_copy(
            src_ref=part, dst_ref=part, send_sem=send_rc.at[src], recv_sem=recv_rc.at[src],
            device_id={"ctx": me + 1}, device_id_type=MESH)

    def fresh_right(src):
        part = kv.at[src, :, :, pl.ds(cached, toks)]
        return pltpu.make_async_remote_copy(
            src_ref=part, dst_ref=part, send_sem=send_rf.at[src], recv_sem=recv_rf.at[src],
            device_id={"ctx": me + 1}, device_id_type=MESH)

    def cached_left(src):
        part = kv.at[src, :, :, pl.ds(0, cached)]
        return pltpu.make_async_remote_copy(
            src_ref=part, dst_ref=part, send_sem=send_lc.at[src], recv_sem=recv_lc.at[src],
            device_id={"ctx": me - 1}, device_id_type=MESH)

    step = 128
    load_k.wait()
    load_v.wait()
    for h in range(heads):
        pick = (iota((step, step * heads), 1) == iota((step, step * heads), 0) * heads + h)
        pick = pick.astype(F32).astype(BF16)
        for c in range(2):
            for b in range(cached // step):
                block = raw[c, pl.ds(b * step * heads, step * heads), :]
                kv[me, h, c, pl.ds(b * step, step), :] = dot(pick, block).astype(BF16)

    pl.semaphore_wait(barrier, neighbours)

    @pl.when(me < n - 1)
    def _():
        cached_right(me).start()

    @pl.when(me > 0)
    def _():
        cached_left(me).start()

    load_t.wait()
    load_d.wait()
    slot = slot_ref[...]
    own = dot(down_v[...], tok_v[...], 1, 1).astype(BF16).astype(F32)
    part = jnp.zeros((width, toks), F32)
    for k in range(own_slots):
        part = part + jnp.where(slot == rep * own_slots + k, own[k * width:(k + 1) * width], 0.0)
    xch[0] = part
    swap = pltpu.make_async_remote_copy(
        src_ref=xch.at[0], dst_ref=xch.at[1], send_sem=send_x, recv_sem=recv_x,
        device_id={"rep": 1 - rep}, device_id_type=MESH)
    swap.start()
    swap.wait_recv()
    shrunk = part + xch[1]

    def spread(rows):
        return jnp.concatenate(
            [jnp.where(slot == s, rows, 0.0) for s in range(slots)], axis=0).astype(BF16)

    def expand(cols_each):
        shape = (slots * rank, slots * rank * cols_each)
        first = iota(shape, 0) * cols_each
        col = iota(shape, 1)
        return ((col >= first) & (col < first + cols_each)).astype(F32).astype(BF16)

    akv = akv_ref[...]
    kvb = kvb_ref[...]
    each = 2 * heads
    for c in range(2):
        wide = dot(spread(shrunk[rank * (1 + c):rank * (2 + c)]), expand(each), 0, 0)
        for h in range(heads):
            keep = lax.rem(iota(wide.shape, 1), each) == c * heads + h
            delta = dot(jnp.where(keep, wide, 0.0).astype(BF16), akv)
            shape = (toks, toks * each)
            pick = (iota(shape, 1) == iota(shape, 0) * each + c * heads + h)
            base = dot(pick.astype(F32).astype(BF16), kvb)
            kv[me, h, c, pl.ds(cached, toks), :] = (base + delta).astype(BF16)

    @pl.when(me < n - 1)
    def _():
        fresh_right(me).start()

    each = heads * groups
    wide = dot(spread(shrunk[0:rank]), expand(each), 0, 0)
    wide = jnp.broadcast_to(wide[:, None, :], (toks, groups, wide.shape[1]))
    wide = wide.reshape(q_rows, wide.shape[2])
    aq = aq_ref[...]
    base_all = qb_ref[...].astype(F32).reshape(toks, each, hd)
    for h in range(heads):
        keep = lax.rem(iota(wide.shape, 1), each) == h * groups + lax.rem(iota(wide.shape, 0), groups)
        delta = dot(jnp.where(keep, wide, 0.0).astype(BF16), aq)
        base = base_all[:, h * groups:(h + 1) * groups].reshape(q_rows, hd)
        q[h] = (base + delta).astype(BF16)

    top[...] = jnp.full(top.shape, FILL, F32)
    total[...] = jnp.zeros(total.shape, F32)
    acc[...] = jnp.zeros(acc.shape, F32)
    tiles = q_rows // TILE
    scale = hd ** -0.5

    def process(src, rows, causal):
        limit = len_ref[src]

        def body(index, carry):
            h = index // tiles
            j = index % tiles
            cols = pl.ds(pl.multiple_of(j * TILE, TILE), TILE)
            scores = dot(kv[src, h, 0, pl.ds(0, rows), :], q[h, cols, :], 1, 1) * scale
            row = iota(scores.shape, 0)
            seen = row < limit
            if rows > cached:
                if causal:
                    token = lax.div(j * TILE + iota(scores.shape, 1), groups)
                    seen = seen & (row < cached) | (row >= cached) & (row - cached <= token)
                else:
                    seen = seen | (row >= cached)
            scores = jnp.where(seen, scores, FILL)
            old = top[h, :, cols]
            new = jnp.maximum(old, jnp.max(scores, axis=0, keepdims=True))
            weights = jnp.exp(scores - new)
            factor = jnp.exp(old - new)
            top[h, :, cols] = new
            total[h, :, cols] = total[h, :, cols] * factor + jnp.sum(weights, axis=0, keepdims=True)
            acc[h, :, cols] = acc[h, :, cols] * factor + dot(
                kv[src, h, 1, pl.ds(0, rows), :], weights.astype(BF16), 0, 0)
            return carry

        lax.fori_loop(0, heads * tiles, body, 0)

    process(me, rows_all, True)

    def arrive(t, carry):
        @pl.when(me - t >= 0)
        def _():
            cached_right(me - t).wait_recv()

            @pl.when(me < n - 1)
            def _():
                cached_right(me - t).start()

            fresh_right(me - t).wait_recv()

            @pl.when(me < n - 1)
            def _():
                fresh_right(me - t).start()

        @pl.when(me + t < n)
        def _():
            cached_left(me + t).wait_recv()

            @pl.when(me > 0)
            def _():
                cached_left(me + t).start()

        @pl.when(me - t >= 0)
        def _():
            process(me - t, rows_all, False)

        @pl.when(me + t < n)
        def _():
            process(me + t, cached, False)

        return carry

    lax.fori_loop(1, n, arrive, 0)

    results = []
    for h in range(heads):
        result = (acc[h] / total[h]).T
        results.append(result.reshape(toks, groups, hd))
    result = jnp.concatenate(results, axis=1) if heads > 1 else results[0]
    out_ref[...] = result.reshape(toks * heads * groups, hd).astype(BF16)

    swap.wait_send()

    def drain(t, carry):
        @pl.when((me - t >= 0) & (me < n - 1))
        def _():
            cached_right(me - t).wait_send()
            fresh_right(me - t).wait_send()

        @pl.when((me + t < n) & (me > 0))
        def _():
            cached_left(me + t).wait_send()

        return carry

    lax.fori_loop(0, n, drain, 0)


def per_device(
    tokens, adapter_down, adapter_query, adapter_keyvalue, query_base, keyvalue_base,
    cached_keys, cached_values, adapter_slot, cached_length,
):
    n = cached_length.shape[0]
    toks, depth = tokens.shape
    slots, rank, heads, groups, hd = adapter_query.shape
    cached = cached_keys.shape[0]
    down = jnp.swapaxes(adapter_down, 1, 2).reshape(-1, depth)
    vmem = pl.BlockSpec(memory_space=pltpu.VMEM)
    hbm = pl.BlockSpec(memory_space=pl.ANY)
    smem = pl.BlockSpec(memory_space=pltpu.SMEM)
    dma = pltpu.SemaphoreType.DMA
    q_rows = toks * groups
    out = pl.pallas_call(
        functools.partial(kernel, n, heads, groups, slots, rank),
        out_shape=jax.ShapeDtypeStruct((toks * heads * groups, hd), BF16),
        in_specs=[hbm, hbm, vmem, vmem, vmem, vmem, hbm, hbm, vmem, smem],
        out_specs=vmem,
        scratch_shapes=[
            pltpu.VMEM((toks, depth), BF16),
            pltpu.VMEM(down.shape, BF16),
            pltpu.VMEM((2, cached * heads, hd), BF16),
            pltpu.VMEM((n, heads, 2, cached + toks, hd), BF16),
            pltpu.VMEM((heads, q_rows, hd), BF16),
            pltpu.VMEM((heads, hd, q_rows), F32),
            pltpu.VMEM((heads, 1, q_rows), F32),
            pltpu.VMEM((heads, 1, q_rows), F32),
            pltpu.VMEM((2, 3 * rank, toks), F32),
            dma((4,)),
            dma((n,)), dma((n,)), dma((n,)), dma((n,)), dma((n,)), dma((n,)), dma, dma,
        ],
        compiler_params=pltpu.CompilerParams(
            collective_id=0, has_side_effects=True, vmem_limit_bytes=48 * 1024 * 1024),
    )(
        tokens, down,
        adapter_query.reshape(-1, hd), adapter_keyvalue.reshape(-1, hd),
        query_base.reshape(-1, hd), keyvalue_base.reshape(-1, hd),
        cached_keys.reshape(-1, hd), cached_values.reshape(-1, hd),
        adapter_slot, cached_length,
    )
    return out.reshape(toks, heads, groups, hd)


def solution(mesh):
    in_specs = (
        P(("group", "ctx"), None),
        P(("group", "ctx", "rep"), None, None),
        P(("group", "ctx"), None, ("tp", "rep"), None, None),
        P(("group", "ctx"), None, None, ("tp", "rep"), None),
        P(("group", "ctx"), ("tp", "rep"), None, None),
        P(("group", "ctx"), None, ("tp", "rep"), None),
        P(("group", "ctx"), ("tp", "rep"), None),
        P(("group", "ctx"), ("tp", "rep"), None),
        P(("group", "ctx"), None),
        P("group"),
    )
    out_specs = P(("group", "ctx"), ("tp", "rep"), None, None)
    return jax.shard_map(
        per_device, mesh=mesh, in_specs=in_specs, out_specs=out_specs, check_vma=False
    )
```

```python
import functools

import jax
import jax.numpy as jnp
from jax import lax
from jax.experimental import pallas as pl
from jax.experimental.pallas import tpu as pltpu
from jax.sharding import PartitionSpec as P

FILL = -1e30
MESH = pl.DeviceIdType.MESH
TILE = 256
F32 = jnp.float32
BF16 = jnp.bfloat16


def iota(shape, dim):
    return lax.broadcasted_iota(jnp.int32, shape, dim)


def dot(a, b, ca=1, cb=0):
    return lax.dot_general(a, b, (((ca,), (cb,)), ((), ())), preferred_element_type=F32)


def kernel(
    n, heads, groups, slots, rank,
    tok_hbm, down_hbm, aq_hbm, akv_hbm, qb_hbm, kvb_hbm, ck_hbm, cv_hbm, slot_hbm, len_hbm,
    out_ref,
    tok_v, down_v, raw, aq_ref, akv_ref, qb_ref, kvb_ref, slot_ref, len_ref,
    kv, q, acc, top, total, xch, local_sem,
    send_rc, recv_rc, send_rf, recv_rf, send_lc, recv_lc, send_x, recv_x,
):
    me = lax.axis_index("ctx")
    rep = lax.axis_index("rep")
    toks = tok_v.shape[0]
    cached = ck_hbm.shape[0] // heads
    rows_all = cached + toks
    width = 3 * rank
    own_slots = down_hbm.shape[0] // width
    hd = q.shape[2]
    q_rows = toks * groups

    load_k = pltpu.make_async_copy(ck_hbm, raw.at[0], local_sem.at[0])
    load_v = pltpu.make_async_copy(cv_hbm, raw.at[1], local_sem.at[1])
    load_t = pltpu.make_async_copy(tok_hbm, tok_v, local_sem.at[2])
    load_d = pltpu.make_async_copy(down_hbm, down_v, local_sem.at[3])
    loads = [load_k, load_v, load_t, load_d]
    small = [
        pltpu.make_async_copy(source, target, local_sem.at[4 + i])
        for i, (source, target) in enumerate((
            (slot_hbm, slot_ref), (len_hbm, len_ref), (akv_hbm, akv_ref), (kvb_hbm, kvb_ref),
            (aq_hbm, aq_ref), (qb_hbm, qb_ref)))
    ]
    for load in loads + small:
        load.start()

    barrier = pltpu.get_barrier_semaphore()
    pl.semaphore_signal(barrier, inc=1, device_id={"rep": 1 - rep}, device_id_type=MESH)

    @pl.when(me > 0)
    def _():
        pl.semaphore_signal(barrier, inc=1, device_id={"ctx": me - 1}, device_id_type=MESH)

    @pl.when(me < n - 1)
    def _():
        pl.semaphore_signal(barrier, inc=1, device_id={"ctx": me + 1}, device_id_type=MESH)

    neighbours = 1 + jnp.where(me > 0, 1, 0) + jnp.where(me < n - 1, 1, 0)

    def cached_right(src):
        part = kv.at[src, :, :, pl.ds(0, cached)]
        return pltpu.make_async_remote_copy(
            src_ref=part, dst_ref=part, send_sem=send_rc.at[src], recv_sem=recv_rc.at[src],
            device_id={"ctx": me + 1}, device_id_type=MESH)

    def fresh_right(src):
        part = kv.at[src, :, :, pl.ds(cached, toks)]
        return pltpu.make_async_remote_copy(
            src_ref=part, dst_ref=part, send_sem=send_rf.at[src], recv_sem=recv_rf.at[src],
            device_id={"ctx": me + 1}, device_id_type=MESH)

    def cached_left(src):
        part = kv.at[src, :, :, pl.ds(0, cached)]
        return pltpu.make_async_remote_copy(
            src_ref=part, dst_ref=part, send_sem=send_lc.at[src], recv_sem=recv_lc.at[src],
            device_id={"ctx": me - 1}, device_id_type=MESH)

    step = 128
    load_k.wait()
    load_v.wait()
    for h in range(heads):
        pick = (iota((step, step * heads), 1) == iota((step, step * heads), 0) * heads + h)
        pick = pick.astype(F32).astype(BF16)
        for c in range(2):
            for b in range(cached // step):
                block = raw[c, pl.ds(b * step * heads, step * heads), :]
                kv[me, h, c, pl.ds(b * step, step), :] = dot(pick, block).astype(BF16)

    pl.semaphore_wait(barrier, neighbours)

    @pl.when(me < n - 1)
    def _():
        cached_right(me).start()

    @pl.when(me > 0)
    def _():
        cached_left(me).start()

    load_t.wait()
    load_d.wait()
    for load in small:
        load.wait()
    slot = slot_ref[...]
    own = dot(down_v[...], tok_v[...], 1, 1).astype(BF16).astype(F32)
    part = jnp.zeros((width, toks), F32)
    for k in range(own_slots):
        part = part + jnp.where(slot == rep * own_slots + k, own[k * width:(k + 1) * width], 0.0)
    xch[0] = part
    swap = pltpu.make_async_remote_copy(
        src_ref=xch.at[0], dst_ref=xch.at[1], send_sem=send_x, recv_sem=recv_x,
        device_id={"rep": 1 - rep}, device_id_type=MESH)
    swap.start()
    swap.wait_recv()
    shrunk = part + xch[1]

    def spread(rows):
        return jnp.concatenate(
            [jnp.where(slot == s, rows, 0.0) for s in range(slots)], axis=0).astype(BF16)

    def expand(cols_each):
        shape = (slots * rank, slots * rank * cols_each)
        first = iota(shape, 0) * cols_each
        col = iota(shape, 1)
        return ((col >= first) & (col < first + cols_each)).astype(F32).astype(BF16)

    akv = akv_ref[...]
    kvb = kvb_ref[...]
    each = 2 * heads
    for c in range(2):
        wide = dot(spread(shrunk[rank * (1 + c):rank * (2 + c)]), expand(each), 0, 0)
        for h in range(heads):
            keep = lax.rem(iota(wide.shape, 1), each) == c * heads + h
            delta = dot(jnp.where(keep, wide, 0.0).astype(BF16), akv)
            shape = (toks, toks * each)
            pick = (iota(shape, 1) == iota(shape, 0) * each + c * heads + h)
            base = dot(pick.astype(F32).astype(BF16), kvb)
            kv[me, h, c, pl.ds(cached, toks), :] = (base + delta).astype(BF16)

    @pl.when(me < n - 1)
    def _():
        fresh_right(me).start()

    each = heads * groups
    wide = dot(spread(shrunk[0:rank]), expand(each), 0, 0)
    wide = jnp.broadcast_to(wide[:, None, :], (toks, groups, wide.shape[1]))
    wide = wide.reshape(q_rows, wide.shape[2])
    aq = aq_ref[...]
    base_all = qb_ref[...].astype(F32).reshape(toks, each, hd)
    for h in range(heads):
        keep = lax.rem(iota(wide.shape, 1), each) == h * groups + lax.rem(iota(wide.shape, 0), groups)
        delta = dot(jnp.where(keep, wide, 0.0).astype(BF16), aq)
        base = base_all[:, h * groups:(h + 1) * groups].reshape(q_rows, hd)
        q[h] = (base + delta).astype(BF16)

    top[...] = jnp.full(top.shape, FILL, F32)
    total[...] = jnp.zeros(total.shape, F32)
    acc[...] = jnp.zeros(acc.shape, F32)
    tiles = q_rows // TILE
    scale = hd ** -0.5

    def process(src, rows, causal):
        limit = len_ref[src]

        def body(index, carry):
            h = index // tiles
            j = index % tiles
            cols = pl.ds(pl.multiple_of(j * TILE, TILE), TILE)
            scores = dot(kv[src, h, 0, pl.ds(0, rows), :], q[h, cols, :], 1, 1) * scale
            row = iota(scores.shape, 0)
            seen = row < limit
            if rows > cached:
                if causal:
                    token = lax.div(j * TILE + iota(scores.shape, 1), groups)
                    seen = seen & (row < cached) | (row >= cached) & (row - cached <= token)
                else:
                    seen = seen | (row >= cached)
            scores = jnp.where(seen, scores, FILL)
            old = top[h, :, cols]
            new = jnp.maximum(old, jnp.max(scores, axis=0, keepdims=True))
            weights = jnp.exp(scores - new)
            factor = jnp.exp(old - new)
            top[h, :, cols] = new
            total[h, :, cols] = total[h, :, cols] * factor + jnp.sum(weights, axis=0, keepdims=True)
            acc[h, :, cols] = acc[h, :, cols] * factor + dot(
                kv[src, h, 1, pl.ds(0, rows), :], weights.astype(BF16), 0, 0)
            return carry

        lax.fori_loop(0, heads * tiles, body, 0)

    process(me, rows_all, True)

    def arrive(t, carry):
        @pl.when(me - t >= 0)
        def _():
            cached_right(me - t).wait_recv()

            @pl.when(me < n - 1)
            def _():
                cached_right(me - t).start()

            fresh_right(me - t).wait_recv()

            @pl.when(me < n - 1)
            def _():
                fresh_right(me - t).start()

        @pl.when(me + t < n)
        def _():
            cached_left(me + t).wait_recv()

            @pl.when(me > 0)
            def _():
                cached_left(me + t).start()

        @pl.when(me - t >= 0)
        def _():
            process(me - t, rows_all, False)

        @pl.when(me + t < n)
        def _():
            process(me + t, cached, False)

        return carry

    lax.fori_loop(1, n, arrive, 0)

    results = []
    for h in range(heads):
        result = (acc[h] / total[h]).T
        results.append(result.reshape(toks, groups, hd))
    result = jnp.concatenate(results, axis=1) if heads > 1 else results[0]
    out_ref[...] = result.reshape(toks * heads * groups, hd).astype(BF16)

    swap.wait_send()

    def drain(t, carry):
        @pl.when((me - t >= 0) & (me < n - 1))
        def _():
            cached_right(me - t).wait_send()
            fresh_right(me - t).wait_send()

        @pl.when((me + t < n) & (me > 0))
        def _():
            cached_left(me + t).wait_send()

        return carry

    lax.fori_loop(0, n, drain, 0)


def per_device(
    tokens, adapter_down, adapter_query, adapter_keyvalue, query_base, keyvalue_base,
    cached_keys, cached_values, adapter_slot, cached_length,
):
    n = cached_length.shape[0]
    toks, depth = tokens.shape
    slots, rank, heads, groups, hd = adapter_query.shape
    cached = cached_keys.shape[0]
    down = jnp.swapaxes(adapter_down, 1, 2).reshape(-1, depth)
    vmem = pl.BlockSpec(memory_space=pltpu.VMEM)
    hbm = pl.BlockSpec(memory_space=pl.ANY)
    dma = pltpu.SemaphoreType.DMA
    q_rows = toks * groups
    out = pl.pallas_call(
        functools.partial(kernel, n, heads, groups, slots, rank),
        out_shape=jax.ShapeDtypeStruct((toks * heads * groups, hd), BF16),
        in_specs=[hbm] * 10,
        out_specs=vmem,
        scratch_shapes=[
            pltpu.VMEM((toks, depth), BF16),
            pltpu.VMEM(down.shape, BF16),
            pltpu.VMEM((2, cached * heads, hd), BF16),
            pltpu.VMEM((slots * rank * heads * groups, hd), BF16),
            pltpu.VMEM((slots * rank * heads * 2, hd), BF16),
            pltpu.VMEM((toks * heads * groups, hd), BF16),
            pltpu.VMEM((toks * heads * 2, hd), BF16),
            pltpu.VMEM(adapter_slot.shape, jnp.int32),
            pltpu.SMEM(cached_length.shape, jnp.int32),
            pltpu.VMEM((n, heads, 2, cached + toks, hd), BF16),
            pltpu.VMEM((heads, q_rows, hd), BF16),
            pltpu.VMEM((heads, hd, q_rows), F32),
            pltpu.VMEM((heads, 1, q_rows), F32),
            pltpu.VMEM((heads, 1, q_rows), F32),
            pltpu.VMEM((2, 3 * rank, toks), F32),
            dma((10,)),
            dma((n,)), dma((n,)), dma((n,)), dma((n,)), dma((n,)), dma((n,)), dma, dma,
        ],
        compiler_params=pltpu.CompilerParams(
            collective_id=0, has_side_effects=True, vmem_limit_bytes=60 * 1024 * 1024),
    )(
        tokens, down,
        adapter_query.reshape(-1, hd), adapter_keyvalue.reshape(-1, hd),
        query_base.reshape(-1, hd), keyvalue_base.reshape(-1, hd),
        cached_keys.reshape(-1, hd), cached_values.reshape(-1, hd),
        adapter_slot, cached_length,
    )
    return out.reshape(toks, heads, groups, hd)


def solution(mesh):
    in_specs = (
        P(("group", "ctx"), None),
        P(("group", "ctx", "rep"), None, None),
        P(("group", "ctx"), None, ("tp", "rep"), None, None),
        P(("group", "ctx"), None, None, ("tp", "rep"), None),
        P(("group", "ctx"), ("tp", "rep"), None, None),
        P(("group", "ctx"), None, ("tp", "rep"), None),
        P(("group", "ctx"), ("tp", "rep"), None),
        P(("group", "ctx"), ("tp", "rep"), None),
        P(("group", "ctx"), None),
        P("group"),
    )
    out_specs = P(("group", "ctx"), ("tp", "rep"), None, None)
    return jax.shard_map(
        per_device, mesh=mesh, in_specs=in_specs, out_specs=out_specs, check_vma=False
    )
```

```python
import functools

import jax
import jax.numpy as jnp
from jax import lax
from jax.experimental import pallas as pl
from jax.experimental.pallas import tpu as pltpu
from jax.sharding import PartitionSpec as P

FILL = -1e30
MESH = pl.DeviceIdType.MESH
TILE = 256
F32 = jnp.float32
BF16 = jnp.bfloat16


def iota(shape, dim):
    return lax.broadcasted_iota(jnp.int32, shape, dim)


def dot(a, b, ca=1, cb=0):
    return lax.dot_general(a, b, (((ca,), (cb,)), ((), ())), preferred_element_type=F32)


def kernel(
    n, heads, groups, slots, rank,
    tok_hbm, down_hbm, aq_hbm, akv_hbm, qb_hbm, kvb_hbm, ck_hbm, cv_hbm, slot_hbm, len_hbm,
    out_ref,
    tok_v, down_v, raw, aq_ref, akv_ref, qb_ref, kvb_ref, slot_ref, len_ref,
    kv, q, acc, top, total, xch, done, local_sem,
    send_rc, recv_rc, send_rf, recv_rf, send_lc, recv_lc, send_x, recv_x,
    send_q, recv_q, send_f, recv_f, send_o, recv_o,
):
    handed = heads > 1 and n > 3
    me = lax.axis_index("ctx")
    last = n - 1
    at_end = ((me == 0) | (me == last)) & handed
    helper = ((me == 1) | (me == last - 1)) & handed
    inner = jnp.where(me == 0, 1, last - 1)
    outer = jnp.where(me == 1, 0, last)
    rep = lax.axis_index("rep")
    toks = tok_v.shape[0]
    cached = ck_hbm.shape[0] // heads
    rows_all = cached + toks
    width = 3 * rank
    own_slots = down_hbm.shape[0] // width
    hd = q.shape[2]
    q_rows = toks * groups

    load_k = pltpu.make_async_copy(ck_hbm, raw.at[0], local_sem.at[0])
    load_v = pltpu.make_async_copy(cv_hbm, raw.at[1], local_sem.at[1])
    load_t = pltpu.make_async_copy(tok_hbm, tok_v, local_sem.at[2])
    load_d = pltpu.make_async_copy(down_hbm, down_v, local_sem.at[3])
    loads = [load_k, load_v, load_t, load_d]
    small = [
        pltpu.make_async_copy(source, target, local_sem.at[4 + i])
        for i, (source, target) in enumerate((
            (slot_hbm, slot_ref), (len_hbm, len_ref), (akv_hbm, akv_ref), (kvb_hbm, kvb_ref),
            (aq_hbm, aq_ref), (qb_hbm, qb_ref)))
    ]
    for load in loads + small:
        load.start()

    barrier = pltpu.get_barrier_semaphore()
    pl.semaphore_signal(barrier, inc=1, device_id={"rep": 1 - rep}, device_id_type=MESH)

    @pl.when(me > 0)
    def _():
        pl.semaphore_signal(barrier, inc=1, device_id={"ctx": me - 1}, device_id_type=MESH)

    @pl.when(me < n - 1)
    def _():
        pl.semaphore_signal(barrier, inc=1, device_id={"ctx": me + 1}, device_id_type=MESH)

    neighbours = 1 + jnp.where(me > 0, 1, 0) + jnp.where(me < n - 1, 1, 0)

    def hop(part, send, recv, to):
        return pltpu.make_async_remote_copy(
            src_ref=part, dst_ref=part, send_sem=send, recv_sem=recv,
            device_id={"ctx": to}, device_id_type=MESH)

    def cached_right(src, h):
        part = kv.at[src, h, :, pl.ds(0, cached)]
        return hop(part, send_rc.at[src, h], recv_rc.at[src, h], me + 1)

    def fresh_right(src, h):
        part = kv.at[src, h, :, pl.ds(cached, toks)]
        return hop(part, send_rf.at[src, h], recv_rf.at[src, h], me + 1)

    def cached_left(src, h):
        part = kv.at[src, h, :, pl.ds(0, cached)]
        return hop(part, send_lc.at[src, h], recv_lc.at[src, h], me - 1)

    def query_in():
        return pltpu.make_async_remote_copy(
            src_ref=q.at[0], dst_ref=q.at[heads], send_sem=send_q, recv_sem=recv_q,
            device_id={"ctx": inner}, device_id_type=MESH)

    def fresh_in():
        return hop(kv.at[last, 0, :, pl.ds(cached, toks)], send_f, recv_f, inner)

    def result_out():
        return pltpu.make_async_remote_copy(
            src_ref=done.at[0], dst_ref=done.at[1], send_sem=send_o, recv_sem=recv_o,
            device_id={"ctx": outer}, device_id_type=MESH)

    def given(h):
        return handed and h == 0

    def to_right(h):
        return me < (last - 1 if given(h) else last)

    def to_left(h):
        return me > (1 if given(h) else 0)

    def from_left(h):
        return (me > 0) & (me < last) if given(h) else me > 0

    def from_right(h):
        return (me > 0) & (me < last) if given(h) else me < last

    def send_cached(h):
        @pl.when(to_right(h))
        def _():
            cached_right(me, h).start()

        @pl.when(to_left(h))
        def _():
            cached_left(me, h).start()

    step = 128
    load_k.wait()
    load_v.wait()
    for h in range(heads):
        pick = (iota((step, step * heads), 1) == iota((step, step * heads), 0) * heads + h)
        pick = pick.astype(F32).astype(BF16)
        for c in range(2):
            for b in range(cached // step):
                block = raw[c, pl.ds(b * step * heads, step * heads), :]
                kv[me, h, c, pl.ds(b * step, step), :] = dot(pick, block).astype(BF16)
        if h == 0:
            pl.semaphore_wait(barrier, neighbours)
            send_cached(0)
        else:
            @pl.when(jnp.logical_not(at_end))
            def _():
                send_cached(h)

    load_t.wait()
    load_d.wait()
    for load in small:
        load.wait()
    slot = slot_ref[...]
    own = dot(down_v[...], tok_v[...], 1, 1).astype(BF16).astype(F32)
    part = jnp.zeros((width, toks), F32)
    for k in range(own_slots):
        part = part + jnp.where(slot == rep * own_slots + k, own[k * width:(k + 1) * width], 0.0)
    xch[0] = part
    swap = pltpu.make_async_remote_copy(
        src_ref=xch.at[0], dst_ref=xch.at[1], send_sem=send_x, recv_sem=recv_x,
        device_id={"rep": 1 - rep}, device_id_type=MESH)
    swap.start()
    swap.wait_recv()
    shrunk = part + xch[1]

    def spread(rows):
        return jnp.concatenate(
            [jnp.where(slot == s, rows, 0.0) for s in range(slots)], axis=0).astype(BF16)

    def expand(cols_each):
        shape = (slots * rank, slots * rank * cols_each)
        first = iota(shape, 0) * cols_each
        col = iota(shape, 1)
        return ((col >= first) & (col < first + cols_each)).astype(F32).astype(BF16)

    akv = akv_ref[...]
    kvb = kvb_ref[...]
    each = 2 * heads
    for c in range(2):
        wide = dot(spread(shrunk[rank * (1 + c):rank * (2 + c)]), expand(each), 0, 0)
        for h in range(heads):
            keep = lax.rem(iota(wide.shape, 1), each) == c * heads + h
            delta = dot(jnp.where(keep, wide, 0.0).astype(BF16), akv)
            shape = (toks, toks * each)
            pick = (iota(shape, 1) == iota(shape, 0) * each + c * heads + h)
            base = dot(pick.astype(F32).astype(BF16), kvb)
            kv[me, h, c, pl.ds(cached, toks), :] = (base + delta).astype(BF16)

    for h in range(heads):
        if given(h):
            @pl.when(me == last)
            def _():
                fresh_in().start()

        @pl.when(to_right(h) & (jnp.logical_not(at_end) | (h == 0)))
        def _():
            fresh_right(me, h).start()

    each = heads * groups
    wide = dot(spread(shrunk[0:rank]), expand(each), 0, 0)
    wide = jnp.broadcast_to(wide[:, None, :], (toks, groups, wide.shape[1]))
    wide = wide.reshape(q_rows, wide.shape[2])
    aq = aq_ref[...]
    base_all = qb_ref[...].astype(F32).reshape(toks, each, hd)
    for h in range(heads):
        keep = lax.rem(iota(wide.shape, 1), each) == h * groups + lax.rem(iota(wide.shape, 0), groups)
        delta = dot(jnp.where(keep, wide, 0.0).astype(BF16), aq)
        base = base_all[:, h * groups:(h + 1) * groups].reshape(q_rows, hd)
        q[h] = (base + delta).astype(BF16)
        if given(h):
            @pl.when(at_end)
            def _():
                query_in().start()
                for other in range(1, heads):
                    send_cached(other)

                    @pl.when(to_right(other))
                    def _():
                        fresh_right(me, other).start()

    top[...] = jnp.full(top.shape, FILL, F32)
    total[...] = jnp.zeros(total.shape, F32)
    acc[...] = jnp.zeros(acc.shape, F32)
    tiles = q_rows // TILE
    scale = hd ** -0.5

    def process(src, rows, head_of, slot_of, low, high):
        limit = len_ref[src]

        def body(index, carry):
            k = index // tiles
            j = index % tiles
            h = head_of(k)
            slot = slot_of(k)
            asker = jnp.where(slot == heads, outer, me)
            cols = pl.ds(pl.multiple_of(j * TILE, TILE), TILE)
            scores = dot(kv[src, h, 0, pl.ds(0, rows), :], q[slot, cols, :], 1, 1) * scale
            row = iota(scores.shape, 0)
            seen = row < limit
            if rows > cached:
                reach = (asker - src) * toks + lax.div(j * TILE + iota(scores.shape, 1), groups)
                seen = seen & (row < cached) | (row >= cached) & (row - cached <= reach)
            scores = jnp.where(seen, scores, FILL)
            old = top[slot, :, cols]
            new = jnp.maximum(old, jnp.max(scores, axis=0, keepdims=True))
            weights = jnp.exp(scores - new)
            factor = jnp.exp(old - new)
            top[slot, :, cols] = new
            total[slot, :, cols] = total[slot, :, cols] * factor + jnp.sum(
                weights, axis=0, keepdims=True)
            acc[slot, :, cols] = acc[slot, :, cols] * factor + dot(
                kv[src, h, 1, pl.ds(0, rows), :], weights.astype(BF16), 0, 0)
            return carry

        lax.fori_loop(low * tiles, high * tiles, body, 0)

    own = jnp.where(at_end, 1, 0)
    process(me, rows_all, lambda k: k, lambda k: k, own, heads)
    asked = 1 + jnp.where(helper, 1, 0)

    def finished(slot):
        return (acc[slot] / total[slot]).T

    def arrive(t, carry):
        left = me - t
        right = me + t
        for h in range(heads):
            @pl.when(from_left(h) & (left >= 0))
            def _():
                cached_right(left, h).wait_recv()

                @pl.when(to_right(h))
                def _():
                    cached_right(left, h).start()

                fresh_right(left, h).wait_recv()

                @pl.when(to_right(h))
                def _():
                    fresh_right(left, h).start()

            @pl.when(from_right(h) & (right < n))
            def _():
                cached_left(right, h).wait_recv()

                @pl.when(to_left(h))
                def _():
                    cached_left(right, h).start()

            if given(h):
                @pl.when(helper & (t == 1))
                def _():
                    query_in().wait_recv()

                    @pl.when(me == last - 1)
                    def _():
                        fresh_in().wait_recv()

                    process(me, rows_all, lambda k: 0, lambda k: heads, 0, 1)

                    @pl.when(me == last - 1)
                    def _():
                        process(last, rows_all, lambda k: 0, lambda k: heads, 0, 1)

            slot_of = (lambda k: jnp.where(k == 0, 0, heads)) if given(h) else (lambda k: h)
            count = asked if given(h) else 1

            @pl.when(from_left(h) & (left >= 0))
            def _():
                process(left, rows_all, lambda k: h, slot_of, 0, count)

            @pl.when(from_right(h) & (right < n))
            def _():
                many = jnp.where(right == last, 1, count) if given(h) else count
                many = jnp.where(me == last - 1, many, count)
                process(right, cached, lambda k: h, slot_of, 0, many)

            if given(h):
                @pl.when(helper & (t == n - 2))
                def _():
                    done[0] = finished(heads).astype(BF16)
                    result_out().start()

        return carry

    lax.fori_loop(1, n, arrive, 0)

    @pl.when(at_end)
    def _():
        result_out().wait_recv()

    @pl.when(jnp.logical_not(at_end))
    def _():
        done[1] = finished(0).astype(BF16)

    results = [done[1].astype(F32).reshape(toks, groups, hd)]
    for h in range(1, heads):
        results.append(finished(h).reshape(toks, groups, hd))
    result = jnp.concatenate(results, axis=1) if heads > 1 else results[0]
    out_ref[...] = result.reshape(toks * heads * groups, hd).astype(BF16)

    swap.wait_send()
    if handed:
        @pl.when(at_end)
        def _():
            query_in().wait_send()

        @pl.when(me == last)
        def _():
            fresh_in().wait_send()

        @pl.when(helper)
        def _():
            result_out().wait_send()

    def drain(t, carry):
        for h in range(heads):
            @pl.when((me - t >= 0) & to_right(h))
            def _():
                cached_right(me - t, h).wait_send()
                fresh_right(me - t, h).wait_send()

            @pl.when((me + t < n) & to_left(h))
            def _():
                cached_left(me + t, h).wait_send()

        return carry

    lax.fori_loop(0, n, drain, 0)


def per_device(
    tokens, adapter_down, adapter_query, adapter_keyvalue, query_base, keyvalue_base,
    cached_keys, cached_values, adapter_slot, cached_length,
):
    n = cached_length.shape[0]
    toks, depth = tokens.shape
    slots, rank, heads, groups, hd = adapter_query.shape
    cached = cached_keys.shape[0]
    down = jnp.swapaxes(adapter_down, 1, 2).reshape(-1, depth)
    vmem = pl.BlockSpec(memory_space=pltpu.VMEM)
    hbm = pl.BlockSpec(memory_space=pl.ANY)
    dma = pltpu.SemaphoreType.DMA
    q_rows = toks * groups
    out = pl.pallas_call(
        functools.partial(kernel, n, heads, groups, slots, rank),
        out_shape=jax.ShapeDtypeStruct((toks * heads * groups, hd), BF16),
        in_specs=[hbm] * 10,
        out_specs=vmem,
        scratch_shapes=[
            pltpu.VMEM((toks, depth), BF16),
            pltpu.VMEM(down.shape, BF16),
            pltpu.VMEM((2, cached * heads, hd), BF16),
            pltpu.VMEM((slots * rank * heads * groups, hd), BF16),
            pltpu.VMEM((slots * rank * heads * 2, hd), BF16),
            pltpu.VMEM((toks * heads * groups, hd), BF16),
            pltpu.VMEM((toks * heads * 2, hd), BF16),
            pltpu.VMEM(adapter_slot.shape, jnp.int32),
            pltpu.SMEM(cached_length.shape, jnp.int32),
            pltpu.VMEM((n, heads, 2, cached + toks, hd), BF16),
            pltpu.VMEM((heads + 1, q_rows, hd), BF16),
            pltpu.VMEM((heads + 1, hd, q_rows), F32),
            pltpu.VMEM((heads + 1, 1, q_rows), F32),
            pltpu.VMEM((heads + 1, 1, q_rows), F32),
            pltpu.VMEM((2, 3 * rank, toks), F32),
            pltpu.VMEM((2, q_rows, hd), BF16),
            dma((10,)),
            *[dma((n, heads))] * 6, *[dma] * 8,
        ],
        compiler_params=pltpu.CompilerParams(
            collective_id=0, has_side_effects=True, vmem_limit_bytes=60 * 1024 * 1024),
    )(
        tokens, down,
        adapter_query.reshape(-1, hd), adapter_keyvalue.reshape(-1, hd),
        query_base.reshape(-1, hd), keyvalue_base.reshape(-1, hd),
        cached_keys.reshape(-1, hd), cached_values.reshape(-1, hd),
        adapter_slot, cached_length,
    )
    return out.reshape(toks, heads, groups, hd)


def solution(mesh):
    in_specs = (
        P(("group", "ctx"), None),
        P(("group", "ctx", "rep"), None, None),
        P(("group", "ctx"), None, ("tp", "rep"), None, None),
        P(("group", "ctx"), None, None, ("tp", "rep"), None),
        P(("group", "ctx"), ("tp", "rep"), None, None),
        P(("group", "ctx"), None, ("tp", "rep"), None),
        P(("group", "ctx"), ("tp", "rep"), None),
        P(("group", "ctx"), ("tp", "rep"), None),
        P(("group", "ctx"), None),
        P("group"),
    )
    out_specs = P(("group", "ctx"), ("tp", "rep"), None, None)
    return jax.shard_map(
        per_device, mesh=mesh, in_specs=in_specs, out_specs=out_specs, check_vma=False
    )
```

```python
import functools

import jax
import jax.numpy as jnp
from jax import lax
from jax.experimental import pallas as pl
from jax.experimental.pallas import tpu as pltpu
from jax.sharding import PartitionSpec as P

FILL = -1e30
MESH = pl.DeviceIdType.MESH
TILE = 256
ABREAST = 4
LOG2_E = 1.4426950408889634
F32 = jnp.float32
BF16 = jnp.bfloat16


def iota(shape, dim):
    return lax.broadcasted_iota(jnp.int32, shape, dim)


def dot(a, b, ca=1, cb=0):
    return lax.dot_general(a, b, (((ca,), (cb,)), ((), ())), preferred_element_type=F32)


def kernel(
    n, heads, groups, slots, rank,
    tok_hbm, down_hbm, aq_hbm, akv_hbm, qb_hbm, kvb_hbm, ck_hbm, cv_hbm, slot_hbm, len_hbm,
    out_ref,
    tok_v, down_v, raw, aq_ref, akv_ref, qb_ref, kvb_ref, slot_ref, len_ref,
    kv, q, acc, top, total, xch, done, local_sem,
    send_rc, recv_rc, send_rf, recv_rf, send_lc, recv_lc, send_x, recv_x,
    send_q, recv_q, send_f, recv_f, send_o, recv_o,
):
    handed = heads > 1 and n > 3
    me = lax.axis_index("ctx")
    last = n - 1
    at_end = ((me == 0) | (me == last)) & handed
    helper = ((me == 1) | (me == last - 1)) & handed
    inner = jnp.where(me == 0, 1, last - 1)
    outer = jnp.where(me == 1, 0, last)
    rep = lax.axis_index("rep")
    toks = tok_v.shape[0]
    cached = ck_hbm.shape[0] // heads
    rows_all = cached + toks
    width = 3 * rank
    own_slots = down_hbm.shape[0] // width
    hd = q.shape[2]
    q_rows = toks * groups

    load_k = pltpu.make_async_copy(ck_hbm, raw.at[0], local_sem.at[0])
    load_v = pltpu.make_async_copy(cv_hbm, raw.at[1], local_sem.at[1])
    load_t = pltpu.make_async_copy(tok_hbm, tok_v, local_sem.at[2])
    load_d = pltpu.make_async_copy(down_hbm, down_v, local_sem.at[3])
    loads = [load_k, load_v, load_t, load_d]
    small = [
        pltpu.make_async_copy(source, target, local_sem.at[4 + i])
        for i, (source, target) in enumerate((
            (slot_hbm, slot_ref), (len_hbm, len_ref), (akv_hbm, akv_ref), (kvb_hbm, kvb_ref),
            (aq_hbm, aq_ref), (qb_hbm, qb_ref)))
    ]
    for load in loads + small:
        load.start()

    barrier = pltpu.get_barrier_semaphore()
    pl.semaphore_signal(barrier, inc=1, device_id={"rep": 1 - rep}, device_id_type=MESH)

    @pl.when(me > 0)
    def _():
        pl.semaphore_signal(barrier, inc=1, device_id={"ctx": me - 1}, device_id_type=MESH)

    @pl.when(me < n - 1)
    def _():
        pl.semaphore_signal(barrier, inc=1, device_id={"ctx": me + 1}, device_id_type=MESH)

    neighbours = 1 + jnp.where(me > 0, 1, 0) + jnp.where(me < n - 1, 1, 0)

    def hop(part, send, recv, to):
        return pltpu.make_async_remote_copy(
            src_ref=part, dst_ref=part, send_sem=send, recv_sem=recv,
            device_id={"ctx": to}, device_id_type=MESH)

    def cached_right(src, h):
        part = kv.at[src, h, :, pl.ds(0, cached)]
        return hop(part, send_rc.at[src, h], recv_rc.at[src, h], me + 1)

    def fresh_right(src, h):
        part = kv.at[src, h, :, pl.ds(cached, toks)]
        return hop(part, send_rf.at[src, h], recv_rf.at[src, h], me + 1)

    def cached_left(src, h):
        part = kv.at[src, h, :, pl.ds(0, cached)]
        return hop(part, send_lc.at[src, h], recv_lc.at[src, h], me - 1)

    def query_in():
        return pltpu.make_async_remote_copy(
            src_ref=q.at[0], dst_ref=q.at[heads], send_sem=send_q, recv_sem=recv_q,
            device_id={"ctx": inner}, device_id_type=MESH)

    def fresh_in():
        return hop(kv.at[last, 0, :, pl.ds(cached, toks)], send_f, recv_f, inner)

    def result_out():
        return pltpu.make_async_remote_copy(
            src_ref=done.at[0], dst_ref=done.at[1], send_sem=send_o, recv_sem=recv_o,
            device_id={"ctx": outer}, device_id_type=MESH)

    def given(h):
        return handed and h == 0

    def to_right(h):
        return me < (last - 1 if given(h) else last)

    def to_left(h):
        return me > (1 if given(h) else 0)

    def from_left(h):
        return (me > 0) & (me < last) if given(h) else me > 0

    def from_right(h):
        return (me > 0) & (me < last) if given(h) else me < last

    def send_cached(h):
        @pl.when(to_right(h))
        def _():
            cached_right(me, h).start()

        @pl.when(to_left(h))
        def _():
            cached_left(me, h).start()

    step = 128
    load_k.wait()
    load_v.wait()
    for h in range(heads):
        pick = (iota((step, step * heads), 1) == iota((step, step * heads), 0) * heads + h)
        pick = pick.astype(F32).astype(BF16)
        for c in range(2):
            for b in range(cached // step):
                block = raw[c, pl.ds(b * step * heads, step * heads), :]
                kv[me, h, c, pl.ds(b * step, step), :] = dot(pick, block).astype(BF16)
        if h == 0:
            pl.semaphore_wait(barrier, neighbours)
            send_cached(0)
        else:
            @pl.when(jnp.logical_not(at_end))
            def _():
                send_cached(h)

    load_t.wait()
    load_d.wait()
    for load in small:
        load.wait()
    slot = slot_ref[...]
    own = dot(down_v[...], tok_v[...], 1, 1).astype(BF16).astype(F32)
    part = jnp.zeros((width, toks), F32)
    for k in range(own_slots):
        part = part + jnp.where(slot == rep * own_slots + k, own[k * width:(k + 1) * width], 0.0)
    xch[0] = part
    swap = pltpu.make_async_remote_copy(
        src_ref=xch.at[0], dst_ref=xch.at[1], send_sem=send_x, recv_sem=recv_x,
        device_id={"rep": 1 - rep}, device_id_type=MESH)
    swap.start()
    swap.wait_recv()
    shrunk = part + xch[1]

    def spread(rows):
        return jnp.concatenate(
            [jnp.where(slot == s, rows, 0.0) for s in range(slots)], axis=0).astype(BF16)

    def expand(cols_each):
        shape = (slots * rank, slots * rank * cols_each)
        first = iota(shape, 0) * cols_each
        col = iota(shape, 1)
        return ((col >= first) & (col < first + cols_each)).astype(F32).astype(BF16)

    akv = akv_ref[...]
    kvb = kvb_ref[...]
    each = 2 * heads
    for c in range(2):
        wide = dot(spread(shrunk[rank * (1 + c):rank * (2 + c)]), expand(each), 0, 0)
        for h in range(heads):
            keep = lax.rem(iota(wide.shape, 1), each) == c * heads + h
            delta = dot(jnp.where(keep, wide, 0.0).astype(BF16), akv)
            shape = (toks, toks * each)
            pick = (iota(shape, 1) == iota(shape, 0) * each + c * heads + h)
            base = dot(pick.astype(F32).astype(BF16), kvb)
            kv[me, h, c, pl.ds(cached, toks), :] = (base + delta).astype(BF16)

    for h in range(heads):
        if given(h):
            @pl.when(me == last)
            def _():
                fresh_in().start()

        @pl.when(to_right(h) & (jnp.logical_not(at_end) | (h == 0)))
        def _():
            fresh_right(me, h).start()

    each = heads * groups
    wide = dot(spread(shrunk[0:rank]), expand(each), 0, 0)
    wide = jnp.broadcast_to(wide[:, None, :], (toks, groups, wide.shape[1]))
    wide = wide.reshape(q_rows, wide.shape[2])
    aq = aq_ref[...]
    base_all = qb_ref[...].astype(F32).reshape(toks, each, hd)
    for h in range(heads):
        keep = lax.rem(iota(wide.shape, 1), each) == h * groups + lax.rem(iota(wide.shape, 0), groups)
        delta = dot(jnp.where(keep, wide, 0.0).astype(BF16), aq)
        base = base_all[:, h * groups:(h + 1) * groups].reshape(q_rows, hd)
        q[h] = (base + delta).astype(BF16)
        if given(h):
            @pl.when(at_end)
            def _():
                query_in().start()
                for other in range(1, heads):
                    send_cached(other)

                    @pl.when(to_right(other))
                    def _():
                        fresh_right(me, other).start()

    top[...] = jnp.full(top.shape, FILL, F32)
    total[...] = jnp.zeros(total.shape, F32)
    acc[...] = jnp.zeros(acc.shape, F32)
    turns = q_rows // (TILE * ABREAST)
    scale = hd ** -0.5 * LOG2_E

    def process(src, rows, head_of, slot_of, low, high):
        limit = len_ref[src]

        def body(index, carry):
            k = index // turns
            h = head_of(k)
            slot = slot_of(k)
            asker = jnp.where(slot == heads, outer, me)
            starts = [(index % turns * ABREAST + i) * TILE for i in range(ABREAST)]
            spans = [pl.ds(pl.multiple_of(start, TILE), TILE) for start in starts]
            keys = kv[src, h, 0, pl.ds(0, rows), :]
            values = kv[src, h, 1, pl.ds(0, rows), :]
            row = iota((rows, TILE), 0)
            wide = [dot(keys, q[slot, cols, :], 1, 1) for cols in spans]
            for start, cols, scores in zip(starts, spans, wide):
                seen = row < limit
                if rows > cached:
                    reach = (asker - src) * toks + lax.div(
                        start + iota((1, TILE), 1), groups) + cached
                    seen = seen & (row < cached) | (row >= cached) & (row <= reach)
                scores = jnp.where(seen, scores, FILL)
                old = top[slot, :, cols]
                new = jnp.maximum(old, jnp.max(scores, axis=0, keepdims=True))
                weights = jnp.exp2(scores * scale - new * scale)
                factor = jnp.exp2((old - new) * scale)
                top[slot, :, cols] = new
                total[slot, :, cols] = total[slot, :, cols] * factor + jnp.sum(
                    weights, axis=0, keepdims=True)
                acc[slot, :, cols] = acc[slot, :, cols] * factor + dot(
                    values, weights.astype(BF16), 0, 0)
            return carry

        lax.fori_loop(low * turns, high * turns, body, 0)

    own = jnp.where(at_end, 1, 0)
    process(me, rows_all, lambda k: k, lambda k: k, own, heads)
    asked = 1 + jnp.where(helper, 1, 0)

    def finished(slot):
        return (acc[slot] / total[slot]).T

    def arrive(t, carry):
        left = me - t
        right = me + t
        for h in range(heads):
            @pl.when(from_left(h) & (left >= 0))
            def _():
                cached_right(left, h).wait_recv()

                @pl.when(to_right(h))
                def _():
                    cached_right(left, h).start()

                fresh_right(left, h).wait_recv()

                @pl.when(to_right(h))
                def _():
                    fresh_right(left, h).start()

            @pl.when(from_right(h) & (right < n))
            def _():
                cached_left(right, h).wait_recv()

                @pl.when(to_left(h))
                def _():
                    cached_left(right, h).start()

            if given(h):
                @pl.when(helper & (t == 1))
                def _():
                    query_in().wait_recv()

                    @pl.when(me == last - 1)
                    def _():
                        fresh_in().wait_recv()

                    process(me, rows_all, lambda k: 0, lambda k: heads, 0, 1)

                    @pl.when(me == last - 1)
                    def _():
                        process(last, rows_all, lambda k: 0, lambda k: heads, 0, 1)

            slot_of = (lambda k: jnp.where(k == 0, 0, heads)) if given(h) else (lambda k: h)
            count = asked if given(h) else 1

            @pl.when(from_left(h) & (left >= 0))
            def _():
                process(left, rows_all, lambda k: h, slot_of, 0, count)

            @pl.when(from_right(h) & (right < n))
            def _():
                many = jnp.where(right == last, 1, count) if given(h) else count
                many = jnp.where(me == last - 1, many, count)
                process(right, cached, lambda k: h, slot_of, 0, many)

            if given(h):
                @pl.when(helper & (t == n - 2))
                def _():
                    done[0] = finished(heads).astype(BF16)
                    result_out().start()

        return carry

    lax.fori_loop(1, n, arrive, 0)

    @pl.when(at_end)
    def _():
        result_out().wait_recv()

    @pl.when(jnp.logical_not(at_end))
    def _():
        done[1] = finished(0).astype(BF16)

    results = [done[1].astype(F32).reshape(toks, groups, hd)]
    for h in range(1, heads):
        results.append(finished(h).reshape(toks, groups, hd))
    result = jnp.concatenate(results, axis=1) if heads > 1 else results[0]
    out_ref[...] = result.reshape(toks * heads * groups, hd).astype(BF16)

    swap.wait_send()
    if handed:
        @pl.when(at_end)
        def _():
            query_in().wait_send()

        @pl.when(me == last)
        def _():
            fresh_in().wait_send()

        @pl.when(helper)
        def _():
            result_out().wait_send()

    def drain(t, carry):
        for h in range(heads):
            @pl.when((me - t >= 0) & to_right(h))
            def _():
                cached_right(me - t, h).wait_send()
                fresh_right(me - t, h).wait_send()

            @pl.when((me + t < n) & to_left(h))
            def _():
                cached_left(me + t, h).wait_send()

        return carry

    lax.fori_loop(0, n, drain, 0)


def per_device(
    tokens, adapter_down, adapter_query, adapter_keyvalue, query_base, keyvalue_base,
    cached_keys, cached_values, adapter_slot, cached_length,
):
    n = cached_length.shape[0]
    toks, depth = tokens.shape
    slots, rank, heads, groups, hd = adapter_query.shape
    cached = cached_keys.shape[0]
    down = jnp.swapaxes(adapter_down, 1, 2).reshape(-1, depth)
    vmem = pl.BlockSpec(memory_space=pltpu.VMEM)
    hbm = pl.BlockSpec(memory_space=pl.ANY)
    dma = pltpu.SemaphoreType.DMA
    q_rows = toks * groups
    out = pl.pallas_call(
        functools.partial(kernel, n, heads, groups, slots, rank),
        out_shape=jax.ShapeDtypeStruct((toks * heads * groups, hd), BF16),
        in_specs=[hbm] * 10,
        out_specs=vmem,
        scratch_shapes=[
            pltpu.VMEM((toks, depth), BF16),
            pltpu.VMEM(down.shape, BF16),
            pltpu.VMEM((2, cached * heads, hd), BF16),
            pltpu.VMEM((slots * rank * heads * groups, hd), BF16),
            pltpu.VMEM((slots * rank * heads * 2, hd), BF16),
            pltpu.VMEM((toks * heads * groups, hd), BF16),
            pltpu.VMEM((toks * heads * 2, hd), BF16),
            pltpu.VMEM(adapter_slot.shape, jnp.int32),
            pltpu.SMEM(cached_length.shape, jnp.int32),
            pltpu.VMEM((n, heads, 2, cached + toks, hd), BF16),
            pltpu.VMEM((heads + 1, q_rows, hd), BF16),
            pltpu.VMEM((heads + 1, hd, q_rows), F32),
            pltpu.VMEM((heads + 1, 1, q_rows), F32),
            pltpu.VMEM((heads + 1, 1, q_rows), F32),
            pltpu.VMEM((2, 3 * rank, toks), F32),
            pltpu.VMEM((2, q_rows, hd), BF16),
            dma((10,)),
            *[dma((n, heads))] * 6, *[dma] * 8,
        ],
        compiler_params=pltpu.CompilerParams(
            collective_id=0, has_side_effects=True, vmem_limit_bytes=60 * 1024 * 1024),
    )(
        tokens, down,
        adapter_query.reshape(-1, hd), adapter_keyvalue.reshape(-1, hd),
        query_base.reshape(-1, hd), keyvalue_base.reshape(-1, hd),
        cached_keys.reshape(-1, hd), cached_values.reshape(-1, hd),
        adapter_slot, cached_length,
    )
    return out.reshape(toks, heads, groups, hd)


def solution(mesh):
    in_specs = (
        P(("group", "ctx"), None),
        P(("group", "ctx", "rep"), None, None),
        P(("group", "ctx"), None, ("tp", "rep"), None, None),
        P(("group", "ctx"), None, None, ("tp", "rep"), None),
        P(("group", "ctx"), ("tp", "rep"), None, None),
        P(("group", "ctx"), None, ("tp", "rep"), None),
        P(("group", "ctx"), ("tp", "rep"), None),
        P(("group", "ctx"), ("tp", "rep"), None),
        P(("group", "ctx"), None),
        P("group"),
    )
    out_specs = P(("group", "ctx"), ("tp", "rep"), None, None)
    return jax.shard_map(
        per_device, mesh=mesh, in_specs=in_specs, out_specs=out_specs, check_vma=False
    )
```

```python
import functools

import jax
import jax.numpy as jnp
from jax import lax
from jax.experimental import pallas as pl
from jax.experimental.pallas import tpu as pltpu
from jax.sharding import PartitionSpec as P

FILL = -1e30
MESH = pl.DeviceIdType.MESH
TILE = 256
ABREAST = 4
LOG2_E = 1.4426950408889634
F32 = jnp.float32
BF16 = jnp.bfloat16


def iota(shape, dim):
    return lax.broadcasted_iota(jnp.int32, shape, dim)


def dot(a, b, ca=1, cb=0):
    return lax.dot_general(a, b, (((ca,), (cb,)), ((), ())), preferred_element_type=F32)


def kernel(
    n, heads, groups, slots, rank,
    tok_hbm, down_hbm, aq_hbm, akv_hbm, qb_hbm, kvb_hbm, ck_hbm, cv_hbm, slot_hbm, len_hbm,
    out_ref,
    tok_v, down_v, raw, aq_ref, akv_ref, qb_ref, kvb_ref, slot_ref, len_ref,
    kv, q, acc, top, total, xch, done, local_sem,
    send_rc, recv_rc, send_rf, recv_rf, send_lc, recv_lc, send_x, recv_x,
    send_q, recv_q, send_f, recv_f, send_o, recv_o,
):
    handed = heads > 1 and n > 3
    me = lax.axis_index("ctx")
    last = n - 1
    at_end = ((me == 0) | (me == last)) & handed
    helper = ((me == 1) | (me == last - 1)) & handed
    inner = jnp.where(me == 0, 1, last - 1)
    outer = jnp.where(me == 1, 0, last)
    rep = lax.axis_index("rep")
    toks = tok_v.shape[0]
    cached = ck_hbm.shape[0] // heads
    rows_all = cached + toks
    width = 3 * rank
    own_slots = down_hbm.shape[0] // width
    hd = q.shape[2]
    q_rows = toks * groups

    load_k = pltpu.make_async_copy(ck_hbm, raw.at[0], local_sem.at[0])
    load_v = pltpu.make_async_copy(cv_hbm, raw.at[1], local_sem.at[1])
    load_t = pltpu.make_async_copy(tok_hbm, tok_v, local_sem.at[2])
    load_d = pltpu.make_async_copy(down_hbm, down_v, local_sem.at[3])
    loads = [load_k, load_v, load_t, load_d]
    small = [
        pltpu.make_async_copy(source, target, local_sem.at[4 + i])
        for i, (source, target) in enumerate((
            (slot_hbm, slot_ref), (len_hbm, len_ref), (akv_hbm, akv_ref), (kvb_hbm, kvb_ref),
            (aq_hbm, aq_ref), (qb_hbm, qb_ref)))
    ]
    for load in loads + small:
        load.start()

    barrier = pltpu.get_barrier_semaphore()
    pl.semaphore_signal(barrier, inc=1, device_id={"rep": 1 - rep}, device_id_type=MESH)

    @pl.when(me > 0)
    def _():
        pl.semaphore_signal(barrier, inc=1, device_id={"ctx": me - 1}, device_id_type=MESH)

    @pl.when(me < n - 1)
    def _():
        pl.semaphore_signal(barrier, inc=1, device_id={"ctx": me + 1}, device_id_type=MESH)

    neighbours = 1 + jnp.where(me > 0, 1, 0) + jnp.where(me < n - 1, 1, 0)

    def hop(part, send, recv, to):
        return pltpu.make_async_remote_copy(
            src_ref=part, dst_ref=part, send_sem=send, recv_sem=recv,
            device_id={"ctx": to}, device_id_type=MESH)

    def cached_right(src, h):
        part = kv.at[src, h, :, pl.ds(0, cached)]
        return hop(part, send_rc.at[src, h], recv_rc.at[src, h], me + 1)

    def fresh_right(src, h):
        part = kv.at[src, h, :, pl.ds(cached, toks)]
        return hop(part, send_rf.at[src, h], recv_rf.at[src, h], me + 1)

    def cached_left(src, h):
        part = kv.at[src, h, :, pl.ds(0, cached)]
        return hop(part, send_lc.at[src, h], recv_lc.at[src, h], me - 1)

    def query_in():
        return pltpu.make_async_remote_copy(
            src_ref=q.at[0], dst_ref=q.at[heads], send_sem=send_q, recv_sem=recv_q,
            device_id={"ctx": inner}, device_id_type=MESH)

    def fresh_in():
        return hop(kv.at[last, 0, :, pl.ds(cached, toks)], send_f, recv_f, inner)

    def result_out():
        return pltpu.make_async_remote_copy(
            src_ref=done.at[0], dst_ref=done.at[1], send_sem=send_o, recv_sem=recv_o,
            device_id={"ctx": outer}, device_id_type=MESH)

    def given(h):
        return handed and h == 0

    def to_right(h):
        return me < (last - 1 if given(h) else last)

    def to_left(h):
        return me > (1 if given(h) else 0)

    def from_left(h):
        return (me > 0) & (me < last) if given(h) else me > 0

    def from_right(h):
        return (me > 0) & (me < last) if given(h) else me < last

    def send_cached(right, left, h):
        @pl.when(right)
        def _():
            cached_right(me, h).start()

        @pl.when(left)
        def _():
            cached_left(me, h).start()

    step = 128
    load_k.wait()
    load_v.wait()
    for h in range(heads):
        pick = (iota((step, step * heads), 1) == iota((step, step * heads), 0) * heads + h)
        pick = pick.astype(F32).astype(BF16)
        for c in range(2):
            for b in range(cached // step):
                block = raw[c, pl.ds(b * step * heads, step * heads), :]
                kv[me, h, c, pl.ds(b * step, step), :] = dot(pick, block).astype(BF16)
        if h == 0:
            pl.semaphore_wait(barrier, neighbours)
            send_cached(to_right(0), to_left(0), 0)
        else:
            early = jnp.logical_not(at_end)
            ahead = jnp.logical_not(to_right(0)) if handed else True
            send_cached(to_right(h) & early & ahead, to_left(h) & early, h)

    load_t.wait()
    load_d.wait()
    for load in small:
        load.wait()
    slot = slot_ref[...]
    own = dot(down_v[...], tok_v[...], 1, 1).astype(BF16).astype(F32)
    part = jnp.zeros((width, toks), F32)
    for k in range(own_slots):
        part = part + jnp.where(slot == rep * own_slots + k, own[k * width:(k + 1) * width], 0.0)
    xch[0] = part
    swap = pltpu.make_async_remote_copy(
        src_ref=xch.at[0], dst_ref=xch.at[1], send_sem=send_x, recv_sem=recv_x,
        device_id={"rep": 1 - rep}, device_id_type=MESH)
    swap.start()
    swap.wait_recv()
    shrunk = part + xch[1]

    def spread(rows):
        return jnp.concatenate(
            [jnp.where(slot == s, rows, 0.0) for s in range(slots)], axis=0).astype(BF16)

    def expand(cols_each):
        shape = (slots * rank, slots * rank * cols_each)
        first = iota(shape, 0) * cols_each
        col = iota(shape, 1)
        return ((col >= first) & (col < first + cols_each)).astype(F32).astype(BF16)

    akv = akv_ref[...]
    kvb = kvb_ref[...]
    each = 2 * heads
    for c in range(2):
        wide = dot(spread(shrunk[rank * (1 + c):rank * (2 + c)]), expand(each), 0, 0)
        for h in range(heads):
            keep = lax.rem(iota(wide.shape, 1), each) == c * heads + h
            delta = dot(jnp.where(keep, wide, 0.0).astype(BF16), akv)
            shape = (toks, toks * each)
            pick = (iota(shape, 1) == iota(shape, 0) * each + c * heads + h)
            base = dot(pick.astype(F32).astype(BF16), kvb)
            kv[me, h, c, pl.ds(cached, toks), :] = (base + delta).astype(BF16)

    for h in range(heads):
        if given(h):
            @pl.when(me == last)
            def _():
                fresh_in().start()

        @pl.when(to_right(h) & (jnp.logical_not(at_end) | (h == 0)))
        def _():
            fresh_right(me, h).start()

    if handed:
        for h in range(1, heads):
            send_cached(to_right(h) & to_right(0) & jnp.logical_not(at_end), False, h)

    each = heads * groups
    wide = dot(spread(shrunk[0:rank]), expand(each), 0, 0)
    wide = jnp.broadcast_to(wide[:, None, :], (toks, groups, wide.shape[1]))
    wide = wide.reshape(q_rows, wide.shape[2])
    aq = aq_ref[...]
    base_all = qb_ref[...].astype(F32).reshape(toks, each, hd)
    for h in range(heads):
        keep = lax.rem(iota(wide.shape, 1), each) == h * groups + lax.rem(iota(wide.shape, 0), groups)
        delta = dot(jnp.where(keep, wide, 0.0).astype(BF16), aq)
        base = base_all[:, h * groups:(h + 1) * groups].reshape(q_rows, hd)
        q[h] = (base + delta).astype(BF16)
        if given(h):
            @pl.when(at_end)
            def _():
                query_in().start()
                for other in range(1, heads):
                    send_cached(to_right(other), to_left(other), other)

                    @pl.when(to_right(other))
                    def _():
                        fresh_right(me, other).start()

    top[...] = jnp.full(top.shape, FILL, F32)
    total[...] = jnp.zeros(total.shape, F32)
    acc[...] = jnp.zeros(acc.shape, F32)
    turns = q_rows // (TILE * ABREAST)
    scale = hd ** -0.5 * LOG2_E

    def process(src, span, head_of, slot_of, low, high):
        limit = len_ref[src]
        first, rows = span

        def body(index, carry):
            k = index // turns
            h = head_of(k)
            slot = slot_of(k)
            asker = jnp.where(slot == heads, outer, me)
            starts = [(index % turns * ABREAST + i) * TILE for i in range(ABREAST)]
            spans = [pl.ds(pl.multiple_of(start, TILE), TILE) for start in starts]
            keys = kv[src, h, 0, pl.ds(first, rows), :]
            values = kv[src, h, 1, pl.ds(first, rows), :]
            row = first + iota((rows, TILE), 0)
            wide = [dot(keys, q[slot, cols, :], 1, 1) for cols in spans]
            for start, cols, scores in zip(starts, spans, wide):
                seen = row < limit
                if first + rows > cached:
                    reach = (asker - src) * toks + lax.div(
                        start + iota((1, TILE), 1), groups) + cached
                    seen = seen & (row < cached) | (row >= cached) & (row <= reach)
                scores = jnp.where(seen, scores, FILL)
                old = top[slot, :, cols]
                new = jnp.maximum(old, jnp.max(scores, axis=0, keepdims=True))
                weights = jnp.exp2(scores * scale - new * scale)
                factor = jnp.exp2((old - new) * scale)
                top[slot, :, cols] = new
                total[slot, :, cols] = total[slot, :, cols] * factor + jnp.sum(
                    weights, axis=0, keepdims=True)
                acc[slot, :, cols] = acc[slot, :, cols] * factor + dot(
                    values, weights.astype(BF16), 0, 0)
            return carry

        lax.fori_loop(low * turns, high * turns, body, 0)

    both, old_part, new_part = (0, rows_all), (0, cached), (cached, toks)
    own = jnp.where(at_end, 1, 0)
    process(me, both, lambda k: k, lambda k: k, own, heads)

    def mine(src, span, h):
        process(src, span, lambda k: h, lambda k: h, 0, 1)

    def asked(src, span):
        process(src, span, lambda k: 0, lambda k: heads, 0, 1)

    def finished(slot):
        return (acc[slot] / total[slot]).T

    def arrive(t, carry):
        left = me - t
        right = me + t
        across = jnp.where(me == 1, right, left)
        for h in range(heads):
            on_left = from_left(h) & (left >= 0)
            on_right = from_right(h) & (right < n)

            @pl.when(on_left)
            def _():
                cached_right(left, h).wait_recv()

                @pl.when(to_right(h))
                def _():
                    cached_right(left, h).start()

            @pl.when(on_right)
            def _():
                cached_left(right, h).wait_recv()

                @pl.when(to_left(h))
                def _():
                    cached_left(right, h).start()

            if given(h):
                @pl.when(helper & (t > 1) & (t < n - 1))
                def _():
                    asked(across, old_part)
            else:
                @pl.when(on_left)
                def _():
                    mine(left, old_part, h)

            @pl.when(on_left)
            def _():
                fresh_right(left, h).wait_recv()

                @pl.when(to_right(h))
                def _():
                    fresh_right(left, h).start()

            if given(h):
                @pl.when((me == last - 1) & (t > 1) & (t < n - 1))
                def _():
                    asked(across, new_part)

                @pl.when(helper & (t == n - 2))
                def _():
                    done[0] = finished(heads).astype(BF16)
                    result_out().start()

            @pl.when(on_left)
            def _():
                mine(left, both if given(h) else new_part, h)

            @pl.when(on_right)
            def _():
                mine(right, old_part, h)

        if handed:
            @pl.when(helper & (t == 1))
            def _():
                query_in().wait_recv()

                @pl.when(me == last - 1)
                def _():
                    fresh_in().wait_recv()

                asked(me, both)
                asked(outer, both)
                asked(across, both)

        return carry

    lax.fori_loop(1, n, arrive, 0)

    @pl.when(at_end)
    def _():
        result_out().wait_recv()

    @pl.when(jnp.logical_not(at_end))
    def _():
        done[1] = finished(0).astype(BF16)

    results = [done[1].astype(F32).reshape(toks, groups, hd)]
    for h in range(1, heads):
        results.append(finished(h).reshape(toks, groups, hd))
    result = jnp.concatenate(results, axis=1) if heads > 1 else results[0]
    out_ref[...] = result.reshape(toks * heads * groups, hd).astype(BF16)

    swap.wait_send()
    if handed:
        @pl.when(at_end)
        def _():
            query_in().wait_send()

        @pl.when(me == last)
        def _():
            fresh_in().wait_send()

        @pl.when(helper)
        def _():
            result_out().wait_send()

    def drain(t, carry):
        for h in range(heads):
            @pl.when((me - t >= 0) & to_right(h))
            def _():
                cached_right(me - t, h).wait_send()
                fresh_right(me - t, h).wait_send()

            @pl.when((me + t < n) & to_left(h))
            def _():
                cached_left(me + t, h).wait_send()

        return carry

    lax.fori_loop(0, n, drain, 0)


def per_device(
    tokens, adapter_down, adapter_query, adapter_keyvalue, query_base, keyvalue_base,
    cached_keys, cached_values, adapter_slot, cached_length,
):
    n = cached_length.shape[0]
    toks, depth = tokens.shape
    slots, rank, heads, groups, hd = adapter_query.shape
    cached = cached_keys.shape[0]
    down = jnp.swapaxes(adapter_down, 1, 2).reshape(-1, depth)
    vmem = pl.BlockSpec(memory_space=pltpu.VMEM)
    hbm = pl.BlockSpec(memory_space=pl.ANY)
    dma = pltpu.SemaphoreType.DMA
    q_rows = toks * groups
    out = pl.pallas_call(
        functools.partial(kernel, n, heads, groups, slots, rank),
        out_shape=jax.ShapeDtypeStruct((toks * heads * groups, hd), BF16),
        in_specs=[hbm] * 10,
        out_specs=vmem,
        scratch_shapes=[
            pltpu.VMEM((toks, depth), BF16),
            pltpu.VMEM(down.shape, BF16),
            pltpu.VMEM((2, cached * heads, hd), BF16),
            pltpu.VMEM((slots * rank * heads * groups, hd), BF16),
            pltpu.VMEM((slots * rank * heads * 2, hd), BF16),
            pltpu.VMEM((toks * heads * groups, hd), BF16),
            pltpu.VMEM((toks * heads * 2, hd), BF16),
            pltpu.VMEM(adapter_slot.shape, jnp.int32),
            pltpu.SMEM(cached_length.shape, jnp.int32),
            pltpu.VMEM((n, heads, 2, cached + toks, hd), BF16),
            pltpu.VMEM((heads + 1, q_rows, hd), BF16),
            pltpu.VMEM((heads + 1, hd, q_rows), F32),
            pltpu.VMEM((heads + 1, 1, q_rows), F32),
            pltpu.VMEM((heads + 1, 1, q_rows), F32),
            pltpu.VMEM((2, 3 * rank, toks), F32),
            pltpu.VMEM((2, q_rows, hd), BF16),
            dma((10,)),
            *[dma((n, heads))] * 6, *[dma] * 8,
        ],
        compiler_params=pltpu.CompilerParams(
            collective_id=0, has_side_effects=True, vmem_limit_bytes=60 * 1024 * 1024),
    )(
        tokens, down,
        adapter_query.reshape(-1, hd), adapter_keyvalue.reshape(-1, hd),
        query_base.reshape(-1, hd), keyvalue_base.reshape(-1, hd),
        cached_keys.reshape(-1, hd), cached_values.reshape(-1, hd),
        adapter_slot, cached_length,
    )
    return out.reshape(toks, heads, groups, hd)


def solution(mesh):
    in_specs = (
        P(("group", "ctx"), None),
        P(("group", "ctx", "rep"), None, None),
        P(("group", "ctx"), None, ("tp", "rep"), None, None),
        P(("group", "ctx"), None, None, ("tp", "rep"), None),
        P(("group", "ctx"), ("tp", "rep"), None, None),
        P(("group", "ctx"), None, ("tp", "rep"), None),
        P(("group", "ctx"), ("tp", "rep"), None),
        P(("group", "ctx"), ("tp", "rep"), None),
        P(("group", "ctx"), None),
        P("group"),
    )
    out_specs = P(("group", "ctx"), ("tp", "rep"), None, None)
    return jax.shard_map(
        per_device, mesh=mesh, in_specs=in_specs, out_specs=out_specs, check_vma=False
    )
```

```python
import functools

import jax
import jax.numpy as jnp
from jax import lax
from jax.experimental import pallas as pl
from jax.experimental.pallas import tpu as pltpu
from jax.sharding import PartitionSpec as P

FILL = -1e30
MESH = pl.DeviceIdType.MESH
TILE = 256
ABREAST = 4
LOG2_E = 1.4426950408889634
F32 = jnp.float32
BF16 = jnp.bfloat16


def iota(shape, dim):
    return lax.broadcasted_iota(jnp.int32, shape, dim)


def dot(a, b, ca=1, cb=0):
    return lax.dot_general(a, b, (((ca,), (cb,)), ((), ())), preferred_element_type=F32)


def kernel(
    n, heads, groups, slots, rank,
    tok_hbm, down_hbm, aq_hbm, akv_hbm, qb_hbm, kvb_hbm, ck_hbm, cv_hbm, slot_hbm, len_hbm,
    out_ref,
    tok_v, down_v, raw, aq_ref, akv_ref, qb_ref, kvb_ref, slot_ref, len_ref,
    kv, q, acc, top, total, xch, done, local_sem,
    send_rc, recv_rc, send_rf, recv_rf, send_lc, recv_lc, send_x, recv_x,
    send_q, recv_q, send_f, recv_f, send_o, recv_o,
):
    handed = heads > 1 and n > 3
    me = lax.axis_index("ctx")
    last = n - 1
    at_end = ((me == 0) | (me == last)) & handed
    helper = ((me == 1) | (me == last - 1)) & handed
    inner = jnp.where(me == 0, 1, last - 1)
    outer = jnp.where(me == 1, 0, last)
    rep = lax.axis_index("rep")
    toks = tok_v.shape[0]
    cached = ck_hbm.shape[0] // heads
    rows_all = cached + toks
    width = 3 * rank
    own_slots = down_hbm.shape[0] // width
    hd = q.shape[2]
    q_rows = toks * groups

    load_k = pltpu.make_async_copy(ck_hbm, raw.at[0], local_sem.at[0])
    load_v = pltpu.make_async_copy(cv_hbm, raw.at[1], local_sem.at[1])
    load_t = pltpu.make_async_copy(tok_hbm, tok_v, local_sem.at[2])
    load_d = pltpu.make_async_copy(down_hbm, down_v, local_sem.at[3])
    loads = [load_k, load_v, load_t, load_d]
    small = [
        pltpu.make_async_copy(source, target, local_sem.at[4 + i])
        for i, (source, target) in enumerate((
            (slot_hbm, slot_ref), (len_hbm, len_ref), (akv_hbm, akv_ref), (kvb_hbm, kvb_ref),
            (aq_hbm, aq_ref), (qb_hbm, qb_ref)))
    ]
    for load in loads + small:
        load.start()

    barrier = pltpu.get_barrier_semaphore()
    pl.semaphore_signal(barrier, inc=1, device_id={"rep": 1 - rep}, device_id_type=MESH)

    @pl.when(me > 0)
    def _():
        pl.semaphore_signal(barrier, inc=1, device_id={"ctx": me - 1}, device_id_type=MESH)

    @pl.when(me < n - 1)
    def _():
        pl.semaphore_signal(barrier, inc=1, device_id={"ctx": me + 1}, device_id_type=MESH)

    neighbours = 1 + jnp.where(me > 0, 1, 0) + jnp.where(me < n - 1, 1, 0)

    def hop(part, send, recv, to):
        return pltpu.make_async_remote_copy(
            src_ref=part, dst_ref=part, send_sem=send, recv_sem=recv,
            device_id={"ctx": to}, device_id_type=MESH)

    def cached_right(src, h):
        part = kv.at[src, h, :, pl.ds(0, cached)]
        return hop(part, send_rc.at[src, h], recv_rc.at[src, h], me + 1)

    def fresh_right(src, h):
        part = kv.at[src, h, :, pl.ds(cached, toks)]
        return hop(part, send_rf.at[src, h], recv_rf.at[src, h], me + 1)

    def cached_left(src, h):
        part = kv.at[src, h, :, pl.ds(0, cached)]
        return hop(part, send_lc.at[src, h], recv_lc.at[src, h], me - 1)

    def query_in():
        return pltpu.make_async_remote_copy(
            src_ref=q.at[0], dst_ref=q.at[heads], send_sem=send_q, recv_sem=recv_q,
            device_id={"ctx": inner}, device_id_type=MESH)

    def fresh_in():
        return hop(kv.at[last, 0, :, pl.ds(cached, toks)], send_f, recv_f, inner)

    def result_out():
        return pltpu.make_async_remote_copy(
            src_ref=done.at[0], dst_ref=done.at[1], send_sem=send_o, recv_sem=recv_o,
            device_id={"ctx": outer}, device_id_type=MESH)

    def given(h):
        return handed and h == 0

    def to_right(h):
        return me < (last - 1 if given(h) else last)

    def to_left(h):
        return me > (1 if given(h) else 0)

    def from_left(h):
        return (me > 0) & (me < last) if given(h) else me > 0

    def from_right(h):
        return (me > 0) & (me < last) if given(h) else me < last

    def send_cached(right, left, h):
        @pl.when(right)
        def _():
            cached_right(me, h).start()

        @pl.when(left)
        def _():
            cached_left(me, h).start()

    step = 128
    load_k.wait()
    load_v.wait()
    for h in range(heads):
        pick = (iota((step, step * heads), 1) == iota((step, step * heads), 0) * heads + h)
        pick = pick.astype(F32).astype(BF16)
        for c in range(2):
            for b in range(cached // step):
                block = raw[c, pl.ds(b * step * heads, step * heads), :]
                kv[me, h, c, pl.ds(b * step, step), :] = dot(pick, block).astype(BF16)
        if h == 0:
            pl.semaphore_wait(barrier, neighbours)
            send_cached(to_right(0), to_left(0), 0)
        else:
            early = jnp.logical_not(at_end)
            ahead = jnp.logical_not(to_right(0)) if handed else True
            send_cached(to_right(h) & early & ahead, to_left(h) & early, h)

    load_t.wait()
    load_d.wait()
    for load in small:
        load.wait()
    slot = slot_ref[...]
    own = dot(down_v[...], tok_v[...], 1, 1).astype(BF16).astype(F32)
    part = jnp.zeros((width, toks), F32)
    for k in range(own_slots):
        part = part + jnp.where(slot == rep * own_slots + k, own[k * width:(k + 1) * width], 0.0)
    xch[0] = part
    swap = pltpu.make_async_remote_copy(
        src_ref=xch.at[0], dst_ref=xch.at[1], send_sem=send_x, recv_sem=recv_x,
        device_id={"rep": 1 - rep}, device_id_type=MESH)
    swap.start()
    swap.wait_recv()
    shrunk = part + xch[1]

    def spread(rows):
        return jnp.concatenate(
            [jnp.where(slot == s, rows, 0.0) for s in range(slots)], axis=0).astype(BF16)

    def expand(cols_each):
        shape = (slots * rank, slots * rank * cols_each)
        first = iota(shape, 0) * cols_each
        col = iota(shape, 1)
        return ((col >= first) & (col < first + cols_each)).astype(F32).astype(BF16)

    akv = akv_ref[...]
    kvb = kvb_ref[...]
    each = 2 * heads
    for c in range(2):
        wide = dot(spread(shrunk[rank * (1 + c):rank * (2 + c)]), expand(each), 0, 0)
        for h in range(heads):
            keep = lax.rem(iota(wide.shape, 1), each) == c * heads + h
            delta = dot(jnp.where(keep, wide, 0.0).astype(BF16), akv)
            shape = (toks, toks * each)
            pick = (iota(shape, 1) == iota(shape, 0) * each + c * heads + h)
            base = dot(pick.astype(F32).astype(BF16), kvb)
            kv[me, h, c, pl.ds(cached, toks), :] = (base + delta).astype(BF16)

    for h in range(heads):
        if given(h):
            @pl.when(me == last)
            def _():
                fresh_in().start()

        @pl.when(to_right(h) & (jnp.logical_not(at_end) | (h == 0)))
        def _():
            fresh_right(me, h).start()

    if handed:
        for h in range(1, heads):
            send_cached(to_right(h) & to_right(0) & jnp.logical_not(at_end), False, h)

    each = heads * groups
    wide = dot(spread(shrunk[0:rank]), expand(each), 0, 0)
    wide = jnp.broadcast_to(wide[:, None, :], (toks, groups, wide.shape[1]))
    wide = wide.reshape(q_rows, wide.shape[2])
    aq = aq_ref[...]
    base_all = qb_ref[...].astype(F32).reshape(toks, each, hd)
    for h in range(heads):
        keep = lax.rem(iota(wide.shape, 1), each) == h * groups + lax.rem(iota(wide.shape, 0), groups)
        delta = dot(jnp.where(keep, wide, 0.0).astype(BF16), aq)
        base = base_all[:, h * groups:(h + 1) * groups].reshape(q_rows, hd)
        q[h] = (base + delta).astype(BF16)
        if given(h):
            @pl.when(at_end)
            def _():
                query_in().start()
                for other in range(1, heads):
                    send_cached(to_right(other), to_left(other), other)

                    @pl.when(to_right(other))
                    def _():
                        fresh_right(me, other).start()

    top[...] = jnp.full(top.shape, FILL, F32)
    total[...] = jnp.zeros(total.shape, F32)
    acc[...] = jnp.zeros(acc.shape, F32)
    turns = q_rows // (TILE * ABREAST)
    scale = hd ** -0.5 * LOG2_E

    def process(src, span, head_of, slot_of, low, high):
        limit = len_ref[src]
        first, rows = span

        def body(index, carry):
            k = index // turns
            h = head_of(k)
            slot = slot_of(k)
            asker = jnp.where(slot == heads, outer, me)
            starts = [(index % turns * ABREAST + i) * TILE for i in range(ABREAST)]
            spans = [pl.ds(pl.multiple_of(start, TILE), TILE) for start in starts]
            keys = kv[src, h, 0, pl.ds(first, rows), :]
            values = kv[src, h, 1, pl.ds(first, rows), :]
            row = first + iota((rows, TILE), 0)
            wide = [dot(keys, q[slot, cols, :], 1, 1) for cols in spans]
            for start, cols, scores in zip(starts, spans, wide):
                seen = row < limit
                if first + rows > cached:
                    reach = (asker - src) * toks + lax.div(
                        start + iota((1, TILE), 1), groups) + cached
                    seen = seen & (row < cached) | (row >= cached) & (row <= reach)
                scores = jnp.where(seen, scores, FILL)
                old = top[slot, :, cols]
                new = jnp.maximum(old, jnp.max(scores, axis=0, keepdims=True))
                weights = jnp.exp2(scores * scale - new * scale)
                factor = jnp.exp2((old - new) * scale)
                top[slot, :, cols] = new
                total[slot, :, cols] = total[slot, :, cols] * factor + jnp.sum(
                    weights, axis=0, keepdims=True)
                acc[slot, :, cols] = acc[slot, :, cols] * factor + dot(
                    values, weights.astype(BF16), 0, 0)
            return carry

        lax.fori_loop(low * turns, high * turns, body, 0)

    both, old_part, new_part = (0, rows_all), (0, cached), (cached, toks)
    own = jnp.where(at_end, 1, 0)
    process(me, both, lambda k: k, lambda k: k, own, heads)

    def mine(src, span, h):
        process(src, span, lambda k: h, lambda k: h, 0, 1)

    def asked(src, span):
        process(src, span, lambda k: 0, lambda k: heads, 0, 1)

    def finished(slot):
        return (acc[slot] / total[slot]).T

    def arrive(t, carry):
        left = me - t
        right = me + t
        across = jnp.where(me == 1, right, left)
        for h in range(heads):
            on_left = from_left(h) & (left >= 0)
            on_right = from_right(h) & (right < n)

            @pl.when(on_left)
            def _():
                cached_right(left, h).wait_recv()

                @pl.when(to_right(h))
                def _():
                    cached_right(left, h).start()

            @pl.when(on_right)
            def _():
                cached_left(right, h).wait_recv()

                @pl.when(to_left(h))
                def _():
                    cached_left(right, h).start()

            if given(h):
                @pl.when(helper & (t > 1) & (t < n - 1))
                def _():
                    asked(across, old_part)
            else:
                @pl.when(on_left)
                def _():
                    mine(left, old_part, h)

            @pl.when(on_left)
            def _():
                fresh_right(left, h).wait_recv()

                @pl.when(to_right(h))
                def _():
                    fresh_right(left, h).start()

            if given(h):
                @pl.when((me == last - 1) & (t > 1) & (t < n - 1))
                def _():
                    asked(across, new_part)

                @pl.when(helper & (t == n - 2))
                def _():
                    done[0] = finished(heads).astype(BF16)
                    result_out().start()

            @pl.when(on_left)
            def _():
                mine(left, both if given(h) else new_part, h)

            @pl.when(on_right)
            def _():
                mine(right, old_part, h)

        if handed:
            @pl.when(helper & (t == 1))
            def _():
                query_in().wait_recv()

                @pl.when(me == last - 1)
                def _():
                    fresh_in().wait_recv()

                asked(me, both)
                asked(outer, both)

                @pl.when(me == 1)
                def _():
                    asked(across, old_part)

                @pl.when(me == last - 1)
                def _():
                    asked(across, both)

        return carry

    lax.fori_loop(1, n, arrive, 0)

    @pl.when(at_end)
    def _():
        result_out().wait_recv()

    @pl.when(jnp.logical_not(at_end))
    def _():
        done[1] = finished(0).astype(BF16)

    results = [done[1].astype(F32).reshape(toks, groups, hd)]
    for h in range(1, heads):
        results.append(finished(h).reshape(toks, groups, hd))
    result = jnp.concatenate(results, axis=1) if heads > 1 else results[0]
    out_ref[...] = result.reshape(toks * heads * groups, hd).astype(BF16)

    swap.wait_send()
    if handed:
        @pl.when(at_end)
        def _():
            query_in().wait_send()

        @pl.when(me == last)
        def _():
            fresh_in().wait_send()

        @pl.when(helper)
        def _():
            result_out().wait_send()

    def drain(t, carry):
        for h in range(heads):
            @pl.when((me - t >= 0) & to_right(h))
            def _():
                cached_right(me - t, h).wait_send()
                fresh_right(me - t, h).wait_send()

            @pl.when((me + t < n) & to_left(h))
            def _():
                cached_left(me + t, h).wait_send()

        return carry

    lax.fori_loop(0, n, drain, 0)


def per_device(
    tokens, adapter_down, adapter_query, adapter_keyvalue, query_base, keyvalue_base,
    cached_keys, cached_values, adapter_slot, cached_length,
):
    n = cached_length.shape[0]
    toks, depth = tokens.shape
    slots, rank, heads, groups, hd = adapter_query.shape
    cached = cached_keys.shape[0]
    down = jnp.swapaxes(adapter_down, 1, 2).reshape(-1, depth)
    vmem = pl.BlockSpec(memory_space=pltpu.VMEM)
    hbm = pl.BlockSpec(memory_space=pltpu.HBM)
    dma = pltpu.SemaphoreType.DMA
    q_rows = toks * groups
    out = pl.pallas_call(
        functools.partial(kernel, n, heads, groups, slots, rank),
        out_shape=jax.ShapeDtypeStruct((toks * heads * groups, hd), BF16),
        in_specs=[hbm] * 10,
        out_specs=vmem,
        scratch_shapes=[
            pltpu.VMEM((toks, depth), BF16),
            pltpu.VMEM(down.shape, BF16),
            pltpu.VMEM((2, cached * heads, hd), BF16),
            pltpu.VMEM((slots * rank * heads * groups, hd), BF16),
            pltpu.VMEM((slots * rank * heads * 2, hd), BF16),
            pltpu.VMEM((toks * heads * groups, hd), BF16),
            pltpu.VMEM((toks * heads * 2, hd), BF16),
            pltpu.VMEM(adapter_slot.shape, jnp.int32),
            pltpu.SMEM(cached_length.shape, jnp.int32),
            pltpu.VMEM((n, heads, 2, cached + toks, hd), BF16),
            pltpu.VMEM((heads + 1, q_rows, hd), BF16),
            pltpu.VMEM((heads + 1, hd, q_rows), F32),
            pltpu.VMEM((heads + 1, 1, q_rows), F32),
            pltpu.VMEM((heads + 1, 1, q_rows), F32),
            pltpu.VMEM((2, 3 * rank, toks), F32),
            pltpu.VMEM((2, q_rows, hd), BF16),
            dma((10,)),
            *[dma((n, heads))] * 6, *[dma] * 8,
        ],
        compiler_params=pltpu.CompilerParams(
            collective_id=0, has_side_effects=True, vmem_limit_bytes=40 * 1024 * 1024),
    )(
        tokens, down,
        adapter_query.reshape(-1, hd), adapter_keyvalue.reshape(-1, hd),
        query_base.reshape(-1, hd), keyvalue_base.reshape(-1, hd),
        cached_keys.reshape(-1, hd), cached_values.reshape(-1, hd),
        adapter_slot, cached_length,
    )
    return out.reshape(toks, heads, groups, hd)


def solution(mesh):
    in_specs = (
        P(("group", "ctx"), None),
        P(("group", "ctx", "rep"), None, None),
        P(("group", "ctx"), None, ("tp", "rep"), None, None),
        P(("group", "ctx"), None, None, ("tp", "rep"), None),
        P(("group", "ctx"), ("tp", "rep"), None, None),
        P(("group", "ctx"), None, ("tp", "rep"), None),
        P(("group", "ctx"), ("tp", "rep"), None),
        P(("group", "ctx"), ("tp", "rep"), None),
        P(("group", "ctx"), None),
        P("group"),
    )
    out_specs = P(("group", "ctx"), ("tp", "rep"), None, None)
    return jax.shard_map(
        per_device, mesh=mesh, in_specs=in_specs, out_specs=out_specs, check_vma=False
    )
```
